256 devices in a mesh: azim: 32 (over z, y_lo, core), radax: 8 (over x, y_hi).
Axes of the slice: x: 4, y: 4 (y_hi: 2, y_lo: 2; y = y_hi * 2 + y_lo), z: 8, core: 2. Of those that a mesh axis runs over, the one named last changes fastest.
Arguments:
- velocity: float32 [3, 256, 64, 1024], P(None, 'azim', None, 'radax')
- rotor_flux: float32 [256, 1024], P('azim', 'radax'), may hold values from -6 to 6
- correlation_weight: float32 [3, 256, 1024], P(None, 'azim', 'radax'), may hold values from 0.2 to 1
- damping: float32 [256, 64, 1024], P('azim', None, 'radax'), may hold values from 0.5 to 4
- offset: int32 [1], replicated, may hold values from 0 to 255
Outputs:
- new_velocity: float32 [3, 256, 64, 1024], P(None, 'azim', None, 'radax')
- pressure: float32 [256, 64, 1024], P('azim', None, 'radax')
The draws below stay inside these ranges and needn't reach their ends.
All inputs are finite; a program needn't handle non-finite values.
Results may differ from the reference program's by a relative error of at most 0.0001.
Values sent between devices are 32-bit elements; how exact they have to be, the bound alone decides.
No kernel may reach another device: no remote copies, remote signals or barrier semaphores. Data moves between devices by JAX's collectives and lax.ppermute only.
A program may use at most 64 MiB of HBM per device.

```python
import math
import jax
import jax.numpy as jnp

CR = 64
ITERS = 3
NA = 256
NL = 1024


def draw_velocity(key, part):
    key = jax.random.fold_in(key, 7)
    ramp = 1.0 + 2.0 * jnp.arange(NA, dtype=jnp.float32) / NA
    ramp = ramp[None, :, None, None]
    field = jax.random.normal(key, (3, NA, CR, NL), jnp.float32) * ramp
    return field.astype(jnp.float32)


def levels(rng, shape, pieces, low, top_value):
    loudness, own = 1.0, jax.random.fold_in(rng, 6)
    for position, parts in pieces:
        draws = jnp.exp(jax.random.uniform(jax.random.fold_in(own, position), (parts,), jnp.float32, low / len(pieces), top_value / len(pieces)))
        loudness = loudness * jnp.repeat(draws, shape[position] // parts).reshape([-1 if axis == position else 1 for axis in range(len(shape))])
    return loudness


def scatter_about(stream_key, shape, deviation, limit, cuts=(), kind=jnp.bfloat16):
    values = deviation * jax.random.normal(stream_key, shape, jnp.float32)
    if cuts:
        values = values * levels(stream_key, shape, cuts, -0.22, 0.18)
    return jnp.clip(values, -limit, limit).astype(kind)


def setup_inputs(seed: int = 0) -> dict:
    key_list = jax.random.split(jax.random.key(seed), 6)
    return {
        "velocity": draw_velocity(jax.random.fold_in(key_list[5], 71), 0),
        "rotor_flux": scatter_about(key_list[1], (NA, NL), 1.0, 6.0, ((0, 32), (1, 8)), jnp.float32),
        "correlation_weight": jnp.clip(0.2 + 0.8 * jax.random.uniform(key_list[2], (3, NA, NL), jnp.float32) ** levels(key_list[2], (3, NA, NL), ((1, 32), (2, 8)), -0.2, 0.2), 0.2, 1.0),
        "damping": jnp.clip(jnp.exp(math.log(4.0) - 2.0794415 * jax.random.uniform(key_list[3], (NA, CR, NL), jnp.float32) ** levels(key_list[3], (NA, CR, NL), ((0, 32), (2, 8)), -0.2, 0.2)), 0.5, 4.0),
        "offset": jax.random.randint(key_list[4], (1,), 0, NA).astype(jnp.int32),
    }


viscosity = 0.1
courant = 0.2


def stencil_parts(grown, inner):
    center = grown[:, 1:-1, :, 1:-1]
    east = grown[:, 2:, :, 1:-1]
    west = grown[:, :-2, :, 1:-1]
    above = grown[:, 1:-1, :, 2:]
    below = grown[:, 1:-1, :, :-2]
    outer = jnp.zeros_like(center[:, :, :1])
    radial = jnp.concatenate([inner[:, :, None, :], center, outer], axis=2)
    return center, east, west, radial[:, :, 2:], radial[:, :, :-2], above, below


def extend(field, inner):
    grown = jnp.concatenate([field[:, -1:], field, field[:, :1]], axis=1)
    grown = jnp.pad(grown, ((0, 0), (0, 0), (0, 0), (1, 1)))
    return stencil_parts(grown, inner)


def reference(velocity, rotor_flux, correlation_weight, damping, offset):
    rotated = jnp.roll(rotor_flux, offset[0], axis=0)
    cyclic = jnp.concatenate([rotated[-1:], rotated, rotated[:1]], axis=0)
    face_flux = correlation_weight[0] * cyclic[:-2] + correlation_weight[1] * cyclic[1:-1] + correlation_weight[2] * cyclic[2:]
    zero_face = jnp.zeros_like(face_flux)
    inner = jnp.stack([zero_face, face_flux, zero_face])
    center, east, west, outward, inward, above, below = extend(velocity, inner)
    nearby = east + west + outward + inward + above + below
    predicted = center + viscosity * (nearby - 6.0 * center) - courant * center[0:1] * 0.5 * (east - west)
    center, east, west, outward, inward, above, below = extend(predicted, inner)
    source = 0.5 * (east[0] - west[0] + outward[1] - inward[1] + above[2] - below[2])
    blank = jnp.zeros((1,) + face_flux.shape, jnp.float32)

    def operate(field):
        center, east, west, outward, inward, above, below = extend(field[None], blank)
        return ((6.0 + damping) * center[0]) - (east + west + outward + inward + above + below)[0]

    pressure = jnp.zeros_like(source)
    residual = source
    direction = source
    norm_now = jnp.sum(residual * residual)
    for step in range(ITERS):
        image = operate(direction)
        alpha = norm_now / jnp.sum(direction * image)
        pressure = pressure + alpha * direction
        residual = residual - alpha * image
        norm_next = jnp.sum(residual * residual)
        direction = residual + (norm_next / norm_now) * direction
        norm_now = norm_next
    center, east, west, outward, inward, above, below = extend(pressure[None], blank)
    gradient = jnp.stack([0.5 * (east - west)[0], 0.5 * (outward - inward)[0], 0.5 * (above - below)[0]])
    return predicted - gradient, pressure
```

```python
import jax
import jax.numpy as jnp
from jax import lax
from jax.experimental import pallas as pl
from jax.experimental.pallas import tpu as pltpu
from jax.sharding import PartitionSpec as P


CENTER = 8.0
HALO = 5
STRIP = 8
GROUP = 2 * STRIP
LANES = 128
VMEM_LIMIT = 48 * 1024 * 1024
DEPTHS = (5, 4, 4, 2)
STARTS = (0, 5, 9, 13)
PLANES = 15


def iota(shape, dim):
    return lax.broadcasted_iota(jnp.int32, shape, dim)


def pack_kernel(velocity, damping, weight, rotor, low, high, edge):
    cells = velocity.shape[1]
    rows = velocity.shape[2]
    fields = [velocity.at[0], velocity.at[1], velocity.at[2], damping]
    for field, depth, start in zip(fields, DEPTHS, STARTS):
        low[start : start + depth] = field[0:depth]
        high[start : start + depth] = field[cells - depth : cells]
    for message in (low, high):
        message[PLANES] = jnp.zeros((rows, LANES), jnp.float32)
        for tap in range(3):
            message[PLANES, tap * cells : (tap + 1) * cells] = weight[tap]
    group = iota((8, LANES), 1) // GROUP
    for number, field in enumerate(fields):

        def plane(p, carry):
            packed = jnp.zeros((8, LANES), jnp.float32)
            for t in range(rows // 8):
                tile = field[p, 8 * t : 8 * t + 8]
                turned = pltpu.roll(tile, (STRIP + GROUP * t) % LANES, 1)
                packed = jnp.where(group == t, turned, packed)
            edge[number * cells + p] = packed
            return carry

        lax.fori_loop(0, cells, plane, 0)
    packed = jnp.zeros((8, LANES), jnp.float32)
    for t, tile in enumerate([weight[0], weight[1], weight[2], rotor[...]]):
        turned = pltpu.roll(tile, STRIP + GROUP * t, 1)
        packed = jnp.where(group == t, turned, packed)
    edge[4 * cells] = packed


def corner_kernel(before, after, rotor, halo, low, high, spread):
    cells = rotor.shape[0]
    left = iota((1, 8, LANES), 2) % GROUP < STRIP
    halo[...] = jnp.where(left, before[...], after[...])
    for number, (depth, start) in enumerate(zip(DEPTHS, STARTS)):
        base = number * cells
        low[start : start + depth] = halo[base : base + depth]
        high[start : start + depth] = halo[base + cells - depth : base + cells]
    low[PLANES] = halo[4 * cells]
    high[PLANES] = halo[4 * cells]
    spread[:, 0:8] = jnp.broadcast_to(rotor[...][None], (spread.shape[0], 8, LANES))
    spread[:, 8:16] = jnp.broadcast_to(halo[4 * cells][None], (spread.shape[0], 8, LANES))


def beside(own, other, lane):
    before = pltpu.roll(jnp.where(lane == LANES - 1, other, own), 1, 1)
    after = pltpu.roll(jnp.where(lane == 0, other, own), LANES - 1, 1)
    return before, after


def across(own, row, inner):
    size = own.shape[0]
    inward = jnp.where(row == 0, inner, pltpu.roll(own, 1, 0))
    outward = jnp.where(row == size - 1, 0.0, pltpu.roll(own, size - 1, 0))
    return inward, outward


def fold(block):
    return jnp.sum(block.reshape(block.shape[0] // 8, 8, LANES), axis=0)


def basis_kernel(
    offset,
    velocity,
    damping,
    weight,
    low,
    high,
    halo,
    low_halo,
    high_halo,
    turned,
    predicted,
    base0,
    base1,
    base2,
    edges,
    sums,
    v0,
    v1,
    v2,
    diag,
    p0,
    p1,
    p2,
    s0,
    s1,
    s2,
    taps,
    rims,
    rot,
    face,
):
    cells, rows = damping.shape[0], damping.shape[1]
    blocks = turned.shape[0]
    total = blocks * cells
    place = lax.axis_index("radax")
    last_place = lax.axis_size("radax") - 1
    lane = iota((rows, LANES), 1)
    row = iota((rows, LANES), 0)
    after_ok = jnp.logical_and(lane < HALO, place < last_place)
    before_ok = jnp.logical_and(lane >= LANES - HALO, place > 0)
    mask = jnp.where(jnp.logical_or(after_ok, before_ok), 1.0, 0.0)
    mask8 = mask[0:8] > 0.5

    grown = ((v0, 0), (v1, 1), (v2, 2))
    for field, number in grown:
        depth, start = DEPTHS[number], STARTS[number]
        field[0, 0:depth] = high[start : start + depth]
        field[0, depth : depth + cells] = velocity[number]
        field[0, depth + cells : 2 * depth + cells] = low[start : start + depth]
    shift = 6.0 - CENTER
    depth, start = DEPTHS[3], STARTS[3]
    diag[0, 0:depth] = high[start : start + depth] + shift
    diag[0, depth : depth + cells] = damping[...] + shift
    diag[0, depth + cells : 2 * depth + cells] = low[start : start + depth] + shift

    def open_strip(packed, field, p):
        for t in range(rows // 8):
            tile = pltpu.roll(packed, (LANES - STRIP - GROUP * t) % LANES, 1)
            field[1, p, 8 * t : 8 * t + 8] = jnp.where(mask8, tile, 0.0)

    for number, field in enumerate((v0, v1, v2, diag)):
        depth, start = DEPTHS[number], STARTS[number]
        extra = shift if number == 3 else 0.0

        def outer(p, carry):
            open_strip(high_halo[start + p] + extra, field, p)
            open_strip(low_halo[start + p] + extra, field, depth + cells + p)
            return carry

        def middle(p, carry):
            open_strip(halo[number * cells + p] + extra, field, depth + p)
            return carry

        lax.fori_loop(0, depth, outer, 0)
        lax.fori_loop(0, cells, middle, 0)

    wide = cells + 6
    for tap in range(3):
        at = tap * cells
        taps[tap, 0:3] = high[PLANES, at + cells - 3 : at + cells]
        taps[tap, 3 : 3 + cells] = weight[tap]
        taps[tap, 3 + cells : wide] = low[PLANES, at : at + 3]
    rims[0:3] = high_halo[PLANES, cells - 3 : cells]
    rims[3 : 3 + cells] = halo[4 * cells]
    rims[3 + cells : wide] = low_halo[PLANES, 0:3]
    first = lax.axis_index("azim") * cells - offset[0] - 4 + 2 * total
    for i in range(wide + 2):
        source = lax.rem(first + i, total)
        block = source // cells
        line = lax.rem(source, cells)
        rot[0, i : i + 1] = turned[block, pl.ds(line, 1)]
        rot[1, i : i + 1] = turned[block, pl.ds(line + 8, 1)]
    own_face = jnp.zeros((wide, LANES), jnp.float32)
    rim_face = jnp.zeros((wide, LANES), jnp.float32)
    rim_taps = rims[0:wide]
    for tap in range(3):
        own_face += taps[tap, 0:wide] * rot[0, tap : tap + wide]
        line = pltpu.roll(rot[1, tap : tap + wide], LANES - 3 * GROUP, 1)
        rim_face += pltpu.roll(rim_taps, (LANES - tap * GROUP) % LANES, 1) * line
    face[0, 0:wide] = own_face
    face[1, 0:wide] = pltpu.roll(rim_face, LANES - STRIP, 1)

    def advance(field, speed, p, q, inner0, inner1):
        x, e = field[0, p + 1], field[1, p + 1]
        out = []
        for tile, (own, other, inner) in enumerate(((x, e, inner0), (e, x, inner1))):
            west, east = field[tile, p], field[tile, p + 2]
            before, after = beside(own, other, lane)
            inward, outward = across(own, row, inner)
            wind = speed[tile, q]
            around = (before + after) + (inward + outward)
            around = around + (east + west) - wind * (east - west)
            out.append(0.4 * own + 0.1 * around)
        return out[0], out[1] * mask

    def first_component(p, carry):
        own, rim = advance(v0, v0, p, p + 1, 0.0, 0.0)
        p0[0, p] = own
        p0[1, p] = rim
        return carry

    def other_components(p, carry):
        f0, f1 = face[0, pl.ds(p, 1)], face[1, pl.ds(p, 1)]
        own, rim = advance(v1, v0, p, p + 2, f0, f1)
        p1[0, p] = own
        p1[1, p] = rim
        own, rim = advance(v2, v0, p, p + 2, 0.0, 0.0)
        p2[0, p] = own
        p2[1, p] = rim
        return carry

    lax.fori_loop(0, cells + 8, first_component, 0)
    lax.fori_loop(0, cells + 6, other_components, 0)

    def divergence(p, carry):
        x, e = p2[0, p], p2[1, p]
        for tile, (own, other) in enumerate(((x, e), (e, x))):
            before, after = beside(own, other, lane)
            inward, outward = across(p1[tile, p], row, face[tile, pl.ds(p, 1)])
            value = 0.5 * (
                (p0[tile, p + 2] - p0[tile, p]) + (outward - inward) + (after - before)
            )
            s0[tile, p] = value if tile == 0 else value * mask
        return carry

    lax.fori_loop(0, cells + 6, divergence, 0)

    def apply(field, p, q, tiles):
        x, e = field[0, p + 1], field[1, p + 1]
        pairs = ((x, e), (e, x))
        out = []
        for tile in range(tiles):
            own, other = pairs[tile]
            before, after = beside(own, other, lane)
            inward, outward = across(own, row, 0.0)
            around = (before + after) + (inward + outward)
            around = around + (field[tile, p + 2] + field[tile, p])
            out.append(diag[tile, q] * own - around)
        return out

    def second(p, carry):
        own, rim = apply(s0, p, p, 2)
        s1[0, p] = own
        s1[1, p] = rim * mask
        return carry

    lax.fori_loop(0, cells + 4, second, 0)

    def third(p, carry):
        own, rim = apply(s1, p, p + 1, 2)
        s2[0, p] = own
        s2[1, p] = rim * mask
        return carry

    lax.fori_loop(0, cells + 2, third, 0)

    def products(p, carry):
        (fourth,) = apply(s2, p, p + 2, 1)
        a, b, c = s0[0, p + 3], s1[0, p + 2], s2[0, p + 1]
        pairs = ((a, a), (a, b), (b, b), (b, c), (c, c), (c, fourth))
        predicted[0, p] = p0[0, p + 4]
        predicted[1, p] = p1[0, p + 3]
        predicted[2, p] = p2[0, p + 3]
        edges[0, p] = s0[1, p + 3]
        edges[1, p] = s1[1, p + 2]
        edges[2, p] = s2[1, p + 1]
        return tuple(t + fold(x * y) for t, (x, y) in zip(carry, pairs))

    zero = jnp.zeros((8, LANES), jnp.float32)
    parts = lax.fori_loop(0, cells, products, (zero,) * 6)
    base0[...] = s0[0, 2 : cells + 4]
    base1[...] = s1[0, 1 : cells + 3]
    base2[...] = s2[0, 0 : cells + 2]

    group = iota((1, LANES), 1) // 16
    line = jnp.zeros((1, LANES), jnp.float32)
    for k, part in enumerate(parts):
        part = jnp.sum(part, axis=0, keepdims=True)
        for step in (64, 32, 16):
            part = part + pltpu.roll(part, step, 1)
        line = jnp.where(group == k, part, line)
    sums[...] = jnp.broadcast_to(line[None], sums.shape)


def coefficients(nu):
    def product(x, y):
        total = 0.0
        for i, a in enumerate(x):
            for j, b in enumerate(y):
                total = total + a * b * nu[i + j]
        return total

    def energy(x):
        total = 0.0
        for i, a in enumerate(x):
            for j, b in enumerate(x):
                total = total + a * b * (nu[i + j + 1] + CENTER * nu[i + j])
        return total

    def image(x):
        out = [CENTER * a for a in x] + [0.0 * x[0]]
        return [out[0]] + [out[i + 1] + x[i] for i in range(len(x))]

    def length(norm, bottom):
        return jnp.clip(norm / bottom, 0.0624, 2.01)

    one = jnp.ones_like(nu[0])
    residual, direction, norm = [one], [one], nu[0]
    answer = [0.0 * one] * 3
    for step in range(3):
        alpha = length(norm, energy(direction))
        answer = [
            a + alpha * direction[i] if i < len(direction) else a for i, a in enumerate(answer)
        ]
        if step == 2:
            break
        moved = image(direction)
        residual = residual + [0.0 * one] * (len(moved) - len(residual))
        residual = [r - alpha * m for r, m in zip(residual, moved)]
        after = product(residual, residual)
        beta = after / norm
        padded = direction + [0.0 * one]
        direction = [r + beta * d for r, d in zip(residual, padded)]
        norm = after
    return answer


def project_kernel(sums, predicted, base0, base1, base2, edges, velocity, pressure, grown):
    cells, rows = pressure.shape[0], pressure.shape[1]
    lane = iota((rows, LANES), 1)
    row = iota((rows, LANES), 0)
    line = jnp.sum(sums[...], axis=0)
    group = iota((1, LANES), 1) // 16
    nu = [
        jnp.sum(jnp.where(group == k, line, 0.0), axis=1, keepdims=True) for k in range(6)
    ]
    c0, c1, c2 = coefficients(nu)

    def combine(p, carry):
        grown[p] = c0 * base0[p] + c1 * base1[p] + c2 * base2[p]
        return carry

    lax.fori_loop(0, cells + 2, combine, 0)

    def gradient(p, carry):
        own = grown[p + 1]
        other = c0 * edges[0, p] + c1 * edges[1, p] + c2 * edges[2, p]
        before, after = beside(own, other, lane)
        inward, outward = across(own, row, 0.0)
        pressure[p] = own
        velocity[0, p] = predicted[0, p] - 0.5 * (grown[p + 2] - grown[p])
        velocity[1, p] = predicted[1, p] - 0.5 * (outward - inward)
        velocity[2, p] = predicted[2, p] - 0.5 * (after - before)
        return carry

    lax.fori_loop(0, cells, gradient, 0)


def call(kernel, shapes, scratch=(), scalars=0, operands=()):
    spec = pl.BlockSpec(memory_space=pltpu.VMEM)
    scalar = pl.BlockSpec(memory_space=pltpu.SMEM)
    specs = [scalar] * scalars + [spec] * (len(operands) - scalars)
    return pl.pallas_call(
        kernel,
        out_shape=[jax.ShapeDtypeStruct(s, jnp.float32) for s in shapes],
        in_specs=specs,
        out_specs=[spec] * len(shapes),
        scratch_shapes=[pltpu.VMEM(s, jnp.float32) for s in scratch],
        compiler_params=pltpu.CompilerParams(vmem_limit_bytes=VMEM_LIMIT),
    )(*operands)


def swap(low, high, axis):
    count = lax.axis_size(axis)
    up = [(i, (i + 1) % count) for i in range(count)]
    down = [(j, i) for i, j in up]
    return lax.ppermute(high, axis, up), lax.ppermute(low, axis, down)


def per_device(velocity, rotor_flux, correlation_weight, damping, offset):
    cells, rows = damping.shape[0], damping.shape[1]
    azim = lax.axis_size("azim")
    devices = azim * lax.axis_size("radax")
    message = (PLANES + 1, rows, LANES)
    strips = (4 * cells + 1, 8, LANES)
    low, high, edge = call(
        pack_kernel,
        [message, message, strips],
        operands=(velocity, damping, correlation_weight, rotor_flux),
    )
    before, after = swap(edge, edge, "radax")
    from_low, from_high = swap(low, high, "azim")
    corner = (PLANES + 1, 8, LANES)
    halo, low, high, spread = call(
        corner_kernel,
        [strips, corner, corner, (azim, 16, LANES)],
        operands=(before, after, rotor_flux),
    )
    low_halo, high_halo = swap(low, high, "azim")
    turned = lax.all_to_all(spread, "azim", 0, 0, tiled=True)
    plane = (rows, LANES)
    own = (cells + 2,) + plane
    predicted, base0, base1, base2, edges, sums = call(
        basis_kernel,
        [(3, cells) + plane, own, own, own, (3, cells) + plane, (devices, 1, LANES)],
        scratch=[
            (2, cells + 10) + plane,
            (2, cells + 8) + plane,
            (2, cells + 8) + plane,
            (2, cells + 4) + plane,
            (2, cells + 8) + plane,
            (2, cells + 6) + plane,
            (2, cells + 6) + plane,
            (2, cells + 6) + plane,
            (2, cells + 4) + plane,
            (2, cells + 2) + plane,
            (3, cells + 8, LANES),
            (cells + 8, LANES),
            (2, cells + 8, LANES),
            (2, cells + 8, LANES),
        ],
        scalars=1,
        operands=(
            offset,
            velocity,
            damping,
            correlation_weight,
            from_high,
            from_low,
            halo,
            high_halo,
            low_halo,
            turned,
        ),
    )
    sums = lax.all_to_all(sums, ("azim", "radax"), 0, 0, tiled=True)
    return call(
        project_kernel,
        [(3, cells) + plane, (cells,) + plane],
        scratch=[own],
        operands=(sums, predicted, base0, base1, base2, edges),
    )


def solution(mesh):
    in_specs = (
        P(None, "azim", None, "radax"),
        P("azim", "radax"),
        P(None, "azim", "radax"),
        P("azim", None, "radax"),
        P(),
    )
    out_specs = (P(None, "azim", None, "radax"), P("azim", None, "radax"))

    def run(*args):
        return tuple(per_device(*args))

    return jax.shard_map(run, mesh=mesh, in_specs=in_specs, out_specs=out_specs, check_vma=False)
```

```python
import jax
import jax.numpy as jnp
from jax import lax
from jax.experimental import pallas as pl
from jax.experimental.pallas import tpu as pltpu
from jax.sharding import PartitionSpec as P


CENTER = 8.0
HALO = 5
STRIP = 8
GROUP = 2 * STRIP
LANES = 128
VMEM_LIMIT = 48 * 1024 * 1024
DEPTHS = (5, 4, 4, 2)
STARTS = (0, 5, 9, 13)
PLANES = 15
PAD = 8


def iota(shape, dim):
    return lax.broadcasted_iota(jnp.int32, shape, dim)


def merge(parts, slot):
    out = parts[0]
    for k, part in enumerate(parts[1:], 1):
        out = jnp.where(slot == k, part, out)
    return out


def spin(tile, steps):
    return pltpu.roll(tile, steps % LANES, 1) if steps % LANES else tile


def edge_kernel(velocity, damping, weight, rotor, to_left, to_right, vel, damp, wt, rt, sems):
    cells, rows = damping.shape[0], damping.shape[1]
    copies = [
        pltpu.make_async_copy(velocity.at[0], vel.at[0], sems.at[0]),
        pltpu.make_async_copy(velocity.at[1], vel.at[1], sems.at[1]),
        pltpu.make_async_copy(velocity.at[2], vel.at[2], sems.at[2]),
        pltpu.make_async_copy(damping, damp, sems.at[3]),
        pltpu.make_async_copy(weight, wt, sems.at[4]),
        pltpu.make_async_copy(rotor, rt, sems.at[5]),
    ]
    for copy in copies:
        copy.start()
    lane = iota((8, LANES), 1)
    group = lane // GROUP
    within = lane % GROUP
    slot = (
        (within >= 4).astype(jnp.int32)
        + (within >= 8).astype(jnp.int32)
        + (within >= 13).astype(jnp.int32)
    )
    fields = [vel.at[0], vel.at[1], vel.at[2], damp]

    def pack(field, p):
        return merge(
            [
                spin(field[p, 8 * t : 8 * t + 8], STRIP + GROUP * t)
                for t in range(rows // 8)
            ],
            group,
        )

    for copy in copies:
        copy.wait()
    for p in range(cells):
        packed = [pack(field, p) for field in fields]
        to_right[p] = merge([spin(x, k) for x, k in zip(packed, (-4, 0, 5, 7))], slot)
        to_left[p] = merge([spin(x, k) for x, k in zip(packed, (-8, -4, 0, 5))], slot)
    tiles = [wt[0], wt[1], wt[2], rt[...]]
    packed = merge([spin(x, STRIP + GROUP * t) for t, x in enumerate(tiles)], group)
    to_right[cells] = packed
    to_left[cells] = packed


def plane_kernel(velocity, damping, weight, order, low, high, sems):
    cells, rows = damping.shape[0], damping.shape[1]
    fields = [velocity.at[0], velocity.at[1], velocity.at[2], damping]
    copies = []
    for field, depth, start in zip(fields, DEPTHS, STARTS):
        copies.append((field.at[0:depth], low.at[start : start + depth]))
        copies.append((field.at[cells - depth : cells], high.at[start : start + depth]))
    for tap in range(3):
        for message in (low, high):
            copies.append((weight.at[tap], message.at[PLANES, tap * cells : (tap + 1) * cells]))
    copies = [
        pltpu.make_async_copy(source, target, sems.at[k])
        for k, (source, target) in enumerate(copies)
    ]
    for copy in copies:
        copy.start()
    for copy in copies:
        copy.wait()


def corner_kernel(before, after, rotor, low, high, spread):
    cells = rotor.shape[0]
    depth = HALO
    for k, side in enumerate((before, after)):
        low[k, 0:depth] = side[0:depth]
        high[k, 0:depth] = side[cells - depth : cells]
    within = iota((8, LANES), 1) % GROUP
    lines = jnp.where(within < STRIP, before[cells], after[cells])
    for message in (low, high):
        message[0, depth] = lines
        message[1, depth] = lines
    own = rotor[...]
    for k in range(spread.shape[0]):
        spread[k, 0:8] = own
        spread[k, 8:16] = lines


def beside(own, other, lane):
    before = pltpu.roll(jnp.where(lane == LANES - 1, other, own), 1, 1)
    after = pltpu.roll(jnp.where(lane == 0, other, own), LANES - 1, 1)
    return before, after


def basis_kernel(
    offset,
    velocity,
    damping,
    weight,
    low,
    high,
    before_own,
    after_own,
    low_halo,
    high_halo,
    turned,
    predicted,
    base0,
    base1,
    base2,
    edges,
    sums,
    v0,
    v1,
    v2,
    diag,
    p0,
    p1,
    p2,
    s0,
    s1,
    s2,
    taps,
    rims,
    rot,
    face,
):
    cells, rows = damping.shape[0], damping.shape[1]
    blocks = turned.shape[0]
    total = blocks * cells
    tiles = range(rows // 8)
    place = lax.axis_index("radax")
    last_place = lax.axis_size("radax") - 1
    lane = iota((8, LANES), 1)
    within = lane % GROUP
    after_ok = jnp.logical_and(lane < HALO, place < last_place)
    before_ok = jnp.logical_and(lane >= LANES - HALO, place > 0)
    keep = jnp.logical_or(after_ok, before_ok)
    zero = jnp.zeros((8, LANES), jnp.float32)

    def at(t, shift=0):
        return slice(PAD + 8 * t + shift, PAD + 8 * t + 8 + shift)

    for field in (v0, v1, v2, p1, s0, s1, s2):
        planes = field.shape[1]
        for tile in range(2):

            def clear(p, carry):
                field[tile, p, 0:PAD] = zero
                field[tile, p, PAD + rows : PAD + rows + PAD] = zero
                return carry

            lax.fori_loop(0, planes, clear, 0, unroll=4)

    body = slice(PAD, PAD + rows)
    for number, field in enumerate((v0, v1, v2)):
        depth, start = DEPTHS[number], STARTS[number]
        for p in range(depth):
            field[0, p, body] = high[start + p]
            field[0, depth + cells + p, body] = low[start + p]

        def fill(p, carry):
            field[0, depth + p, body] = velocity[number, p]
            return carry

        lax.fori_loop(0, cells, fill, 0, unroll=4)
    shift = 6.0 - CENTER
    depth, start = DEPTHS[3], STARTS[3]
    for p in range(depth):
        diag[0, p] = high[start + p] + shift
        diag[0, depth + cells + p] = low[start + p] + shift

    def fill_diag(p, carry):
        diag[0, depth + p] = damping[p] + shift
        return carry

    lax.fori_loop(0, cells, fill_diag, 0, unroll=4)

    turns = ((4, 8), (0, 4), (-5, 0), (-7, -5))

    def open_strips(before, after, plane, numbers):
        for number in numbers:
            field, (a, b) = (v0, v1, v2, diag)[number], turns[number]
            strip = jnp.where(within < STRIP, spin(before, a), spin(after, b))
            q = plane + DEPTHS[number]
            for t in tiles:
                tile = jnp.where(keep, spin(strip, -STRIP - GROUP * t), 0.0)
                if number == 3:
                    field[1, q, 8 * t : 8 * t + 8] = tile + shift
                else:
                    field[1, q, at(t)] = tile

    for k in range(HALO):
        numbers = [n for n in range(4) if DEPTHS[n] >= HALO - k]
        open_strips(high_halo[0, k], high_halo[1, k], k - HALO, numbers)
        numbers = [n for n in range(4) if DEPTHS[n] > k]
        open_strips(low_halo[0, k], low_halo[1, k], cells + k, numbers)

    def middle(p, carry):
        open_strips(before_own[p], after_own[p], p, range(4))
        return carry

    lax.fori_loop(0, cells, middle, 0, unroll=4)

    wide = cells + 6
    for tap in range(3):
        line = tap * cells
        taps[tap, 0:3] = high[PLANES, line + cells - 3 : line + cells]
        taps[tap, 3 : 3 + cells] = weight[tap]
        taps[tap, 3 + cells : wide] = low[PLANES, line : line + 3]
    rims[0:3] = high_halo[0, HALO, cells - 3 : cells]
    rims[3 : 3 + cells] = jnp.where(within < STRIP, before_own[cells], after_own[cells])
    rims[3 + cells : wide] = low_halo[0, HALO, 0:3]
    first = lax.axis_index("azim") * cells - offset[0] - 4 + 2 * total
    for i in range(wide + 2):
        source = lax.rem(first + i, total)
        block = source // cells
        line = lax.rem(source, cells)
        rot[0, i : i + 1] = turned[block, pl.ds(line, 1)]
        rot[1, i : i + 1] = turned[block, pl.ds(line + 8, 1)]
    own_face = jnp.zeros((wide, LANES), jnp.float32)
    rim_face = jnp.zeros((wide, LANES), jnp.float32)
    rim_taps = rims[0:wide]
    for tap in range(3):
        own_face += taps[tap, 0:wide] * rot[0, tap : tap + wide]
        rim_face += spin(rim_taps, -tap * GROUP) * spin(rot[1, tap : tap + wide], -3 * GROUP)
    face[0, 0:wide] = own_face
    face[1, 0:wide] = spin(rim_face, -STRIP)

    def set_face(p, carry):
        for tile in range(2):
            line = face[tile, pl.ds(p, 1)]
            v1[tile, p + 1, PAD - 1 : PAD] = line
            p1[tile, p, PAD - 1 : PAD] = line
        return carry

    lax.fori_loop(0, wide, set_face, 0, unroll=4)

    def pair(field, p, t):
        x, e = field[0, p, at(t)], field[1, p, at(t)]
        return (x, e), (e, x)

    def advance(field, speed, p, q, t):
        out = []
        for tile, (own, other) in enumerate(pair(field, p + 1, t)):
            west, east = field[tile, p, at(t)], field[tile, p + 2, at(t)]
            before, after = beside(own, other, lane)
            inward, outward = field[tile, p + 1, at(t, -1)], field[tile, p + 1, at(t, 1)]
            wind = speed[tile, q, at(t)]
            around = (before + after) + (inward + outward)
            around = around + ((east + west) - wind * (east - west))
            out.append(0.4 * own + 0.1 * around)
        return out[0], jnp.where(keep, out[1], 0.0)

    def first_component(p, carry):
        for t in tiles:
            own, rim = advance(v0, v0, p, p + 1, t)
            p0[0, p, at(t, -PAD)] = own
            p0[1, p, at(t, -PAD)] = rim
        return carry

    def other_components(p, carry):
        for t in tiles:
            own, rim = advance(v1, v0, p, p + 2, t)
            p1[0, p, at(t)] = own
            p1[1, p, at(t)] = rim
            own, rim = advance(v2, v0, p, p + 2, t)
            p2[0, p, at(t, -PAD)] = own
            p2[1, p, at(t, -PAD)] = rim
        return carry

    lax.fori_loop(0, cells + 8, first_component, 0, unroll=4)
    lax.fori_loop(0, cells + 6, other_components, 0)

    def divergence(p, carry):
        for t in tiles:
            x, e = p2[0, p, at(t, -PAD)], p2[1, p, at(t, -PAD)]
            for tile, (own, other) in enumerate(((x, e), (e, x))):
                before, after = beside(own, other, lane)
                inward, outward = p1[tile, p, at(t, -1)], p1[tile, p, at(t, 1)]
                west, east = p0[tile, p, at(t, -PAD)], p0[tile, p + 2, at(t, -PAD)]
                value = 0.5 * ((east - west) + (outward - inward) + (after - before))
                s0[tile, p, at(t)] = value if tile == 0 else jnp.where(keep, value, 0.0)
        return carry

    lax.fori_loop(0, cells + 6, divergence, 0, unroll=4)

    def apply(field, p, q, t, count):
        out = []
        for tile, (own, other) in list(enumerate(pair(field, p + 1, t)))[:count]:
            before, after = beside(own, other, lane)
            inward, outward = field[tile, p + 1, at(t, -1)], field[tile, p + 1, at(t, 1)]
            around = (before + after) + (inward + outward)
            around = around + (field[tile, p + 2, at(t)] + field[tile, p, at(t)])
            out.append(diag[tile, q, at(t, -PAD)] * own - around)
        return out

    def second(p, carry):
        for t in tiles:
            own, rim = apply(s0, p, p, t, 2)
            s1[0, p, at(t)] = own
            s1[1, p, at(t)] = jnp.where(keep, rim, 0.0)
        return carry

    lax.fori_loop(0, cells + 4, second, 0, unroll=4)

    def third(p, carry):
        for t in tiles:
            own, rim = apply(s1, p, p + 1, t, 2)
            s2[0, p, at(t)] = own
            s2[1, p, at(t)] = jnp.where(keep, rim, 0.0)
        return carry

    lax.fori_loop(0, cells + 2, third, 0, unroll=4)

    def products(p, carry):
        for t in tiles:
            (fourth,) = apply(s2, p, p + 2, t, 1)
            a, b, c = s0[0, p + 3, at(t)], s1[0, p + 2, at(t)], s2[0, p + 1, at(t)]
            pairs = ((a, a), (a, b), (b, b), (b, c), (c, c), (c, fourth))
            carry = tuple(s + x * y for s, (x, y) in zip(carry, pairs))
        predicted[0, p] = p0[0, p + 4]
        predicted[1, p] = p1[0, p + 3, body]
        predicted[2, p] = p2[0, p + 3]
        edges[0, p] = s0[1, p + 3, body]
        edges[1, p] = s1[1, p + 2, body]
        edges[2, p] = s2[1, p + 1, body]
        return carry

    parts = lax.fori_loop(0, cells, products, (zero,) * 6)

    def give(p, carry):
        base0[p] = s0[0, p + 2, body]
        base1[p] = s1[0, p + 1, body]
        base2[p] = s2[0, p, body]
        return carry

    lax.fori_loop(0, cells + 2, give, 0, unroll=4)

    group = iota((1, LANES), 1) // 16
    lines = []
    for part in parts:
        part = jnp.sum(part, axis=0, keepdims=True)
        for step in (64, 32, 16):
            part = part + pltpu.roll(part, step, 1)
        lines.append(part)
    sums[...] = jnp.broadcast_to(merge(lines, group)[None], sums.shape)


def across(own, row, inner):
    size = own.shape[0]
    inward = jnp.where(row == 0, inner, pltpu.roll(own, 1, 0))
    outward = jnp.where(row == size - 1, 0.0, pltpu.roll(own, size - 1, 0))
    return inward, outward


def coefficients(nu):
    def product(x, y):
        total = 0.0
        for i, a in enumerate(x):
            for j, b in enumerate(y):
                total = total + a * b * nu[i + j]
        return total

    def energy(x):
        total = 0.0
        for i, a in enumerate(x):
            for j, b in enumerate(x):
                total = total + a * b * (nu[i + j + 1] + CENTER * nu[i + j])
        return total

    def image(x):
        out = [CENTER * a for a in x] + [0.0 * x[0]]
        return [out[0]] + [out[i + 1] + x[i] for i in range(len(x))]

    def length(norm, bottom):
        return jnp.clip(norm / bottom, 0.0624, 2.01)

    one = jnp.ones_like(nu[0])
    residual, direction, norm = [one], [one], nu[0]
    answer = [0.0 * one] * 3
    for step in range(3):
        alpha = length(norm, energy(direction))
        answer = [
            a + alpha * direction[i] if i < len(direction) else a for i, a in enumerate(answer)
        ]
        if step == 2:
            break
        moved = image(direction)
        residual = residual + [0.0 * one] * (len(moved) - len(residual))
        residual = [r - alpha * m for r, m in zip(residual, moved)]
        after = product(residual, residual)
        beta = after / norm
        padded = direction + [0.0 * one]
        direction = [r + beta * d for r, d in zip(residual, padded)]
        norm = after
    return answer


def project_kernel(sums, predicted, base0, base1, base2, edges, velocity, pressure, grown):
    cells, rows = pressure.shape[0], pressure.shape[1]
    lane = iota((rows, LANES), 1)
    row = iota((rows, LANES), 0)
    line = jnp.sum(sums[...], axis=0)
    group = iota((1, LANES), 1) // 16
    nu = [
        jnp.sum(jnp.where(group == k, line, 0.0), axis=1, keepdims=True) for k in range(6)
    ]
    c0, c1, c2 = coefficients(nu)

    def combine(p, carry):
        grown[p] = c0 * base0[p] + c1 * base1[p] + c2 * base2[p]
        return carry

    lax.fori_loop(0, cells + 2, combine, 0)

    def gradient(p, carry):
        own = grown[p + 1]
        other = c0 * edges[0, p] + c1 * edges[1, p] + c2 * edges[2, p]
        before, after = beside(own, other, lane)
        inward, outward = across(own, row, 0.0)
        pressure[p] = own
        velocity[0, p] = predicted[0, p] - 0.5 * (grown[p + 2] - grown[p])
        velocity[1, p] = predicted[1, p] - 0.5 * (outward - inward)
        velocity[2, p] = predicted[2, p] - 0.5 * (after - before)
        return carry

    lax.fori_loop(0, cells, gradient, 0)


def call(kernel, shapes, operands, scratch=(), spaces=None, outs=pltpu.VMEM, sems=0):
    spec = lambda space: pl.BlockSpec(memory_space=space)
    spaces = spaces or [pltpu.VMEM] * len(operands)
    buffers = [pltpu.VMEM(s, jnp.float32) for s in scratch]
    if sems:
        buffers.append(pltpu.SemaphoreType.DMA((sems,)))
    return pl.pallas_call(
        kernel,
        out_shape=[jax.ShapeDtypeStruct(s, jnp.float32) for s in shapes],
        in_specs=[spec(space) for space in spaces],
        out_specs=[spec(outs)] * len(shapes),
        scratch_shapes=buffers,
        compiler_params=pltpu.CompilerParams(vmem_limit_bytes=VMEM_LIMIT),
    )(*operands)


def swap(low, high, axis):
    count = lax.axis_size(axis)
    up = [(i, (i + 1) % count) for i in range(count)]
    down = [(j, i) for i, j in up]
    return lax.ppermute(high, axis, up), lax.ppermute(low, axis, down)


def per_device(velocity, rotor_flux, correlation_weight, damping, offset):
    cells, rows = damping.shape[0], damping.shape[1]
    azim = lax.axis_size("azim")
    devices = azim * lax.axis_size("radax")
    plane = (rows, LANES)
    strips = (cells + 1, 8, LANES)
    to_left, to_right = call(
        edge_kernel,
        [strips, strips],
        (velocity, damping, correlation_weight, rotor_flux),
        scratch=[(3, cells) + plane, (cells,) + plane, (3, cells, LANES), (cells, LANES)],
        spaces=[pltpu.HBM] * 4,
        sems=6,
    )
    before, after = swap(to_left, to_right, "radax")
    message = (PLANES + 1,) + plane
    low, high = call(
        plane_kernel,
        [message, message],
        (velocity, damping, correlation_weight, to_left),
        spaces=[pltpu.HBM] * 3 + [pl.ANY],
        outs=pl.ANY,
        sems=14,
    )
    from_low, from_high = swap(low, high, "azim")
    corner = (2, HALO + 1, 8, LANES)
    low, high, spread = call(
        corner_kernel,
        [corner, corner, (azim, 16, LANES)],
        (before, after, rotor_flux),
    )
    low_halo, high_halo = swap(low, high, "azim")
    turned = lax.all_to_all(spread, "azim", 0, 0, tiled=True)
    own = (cells + 2,) + plane
    high_plane = (rows + 2 * PAD, LANES)
    predicted, base0, base1, base2, edges, sums = call(
        basis_kernel,
        [(3, cells) + plane, own, own, own, (3, cells) + plane, (devices, 1, LANES)],
        (
            offset,
            velocity,
            damping,
            correlation_weight,
            from_high,
            from_low,
            before,
            after,
            high_halo,
            low_halo,
            turned,
        ),
        scratch=[
            (2, cells + 10) + high_plane,
            (2, cells + 8) + high_plane,
            (2, cells + 8) + high_plane,
            (2, cells + 4) + plane,
            (2, cells + 8) + plane,
            (2, cells + 6) + high_plane,
            (2, cells + 6) + plane,
            (2, cells + 6) + high_plane,
            (2, cells + 4) + high_plane,
            (2, cells + 2) + high_plane,
            (3, cells + 8, LANES),
            (cells + 8, LANES),
            (2, cells + 8, LANES),
            (2, cells + 8, LANES),
        ],
        spaces=[pltpu.SMEM] + [pltpu.VMEM] * 10,
    )
    sums = lax.all_to_all(sums, ("azim", "radax"), 0, 0, tiled=True)
    return call(
        project_kernel,
        [(3, cells) + plane, (cells,) + plane],
        (sums, predicted, base0, base1, base2, edges),
        scratch=[own],
    )


def solution(mesh):
    in_specs = (
        P(None, "azim", None, "radax"),
        P("azim", "radax"),
        P(None, "azim", "radax"),
        P("azim", None, "radax"),
        P(),
    )
    out_specs = (P(None, "azim", None, "radax"), P("azim", None, "radax"))

    def run(*args):
        return tuple(per_device(*args))

    return jax.shard_map(run, mesh=mesh, in_specs=in_specs, out_specs=out_specs, check_vma=False)
```

```python
import jax
import jax.numpy as jnp
from jax import lax
from jax.experimental import pallas as pl
from jax.experimental.pallas import tpu as pltpu
from jax.sharding import PartitionSpec as P


CENTER = 8.0
HALO = 5
LANES = 128
HALF = 64
FRONT = 16
TALL = LANES + 2 * FRONT
TILES = LANES // 8
VMEM_LIMIT = 48 * 1024 * 1024
WHOLE_VMEM = 62 * 1024 * 1024
DEPTHS = (5, 4, 4, 2)
STARTS = (0, 5, 9, 13)
PLANES = 15
REACH = (4, 4, 5, 2)
FROM = (0, 4, 8, 13)
STRIP = 16
BODY = slice(FRONT, FRONT + LANES)


def iota(shape, dim):
    return lax.broadcasted_iota(jnp.int32, shape, dim)


def spin(tile, steps):
    return pltpu.roll(tile, steps % LANES, 1) if steps % LANES else tile


def at(t, shift=0):
    start = FRONT - 8 + 8 * t + shift
    return slice(start, start + 8)


def paired(first, second):
    return jnp.concatenate([first, second], axis=0).T


def edge_kernel(velocity, damping, weight, to_left, to_right, vel, damp, wt, turned, sems):
    cells = damping.shape[0]
    pairs = cells // 2
    copies = [pltpu.make_async_copy(damping, damp, sems.at[3])]
    copies += [pltpu.make_async_copy(velocity.at[k], vel.at[k], sems.at[k]) for k in range(3)]
    copies += [pltpu.make_async_copy(weight, wt, sems.at[4])]
    for copy in copies:
        copy.start()
    for copy in copies:
        copy.wait()
    fields = [vel.at[0], vel.at[1], vel.at[2], damp]
    for i in range(pairs):
        base = STRIP * i
        for field, reach, start in zip(fields, REACH, FROM):
            turned[...] = paired(field[i], field[cells - 1 - i])
            rows = slice(base + start, base + start + reach)
            to_left[rows] = turned[0:reach]
            to_right[rows] = turned[LANES - reach : LANES]
        for message in (to_left, to_right):
            message[base + STRIP - 1 : base + STRIP] = jnp.zeros((1, LANES), jnp.float32)
    for tap in range(3):
        rows = slice(STRIP * pairs + tap * cells, STRIP * pairs + (tap + 1) * cells)
        to_left[rows] = wt[tap]
        to_right[rows] = wt[tap]


def plane_kernel(velocity, damping, weight, order, low, high, own):
    cells, rows = damping.shape[0], damping.shape[1]
    fields = [velocity.at[0], velocity.at[1], velocity.at[2], damping]
    for number, (field, depth, start) in enumerate(zip(fields, DEPTHS, STARTS)):
        low[start : start + depth] = field[0:depth]
        high[start : start + depth] = field[cells - depth : cells]
        for i in range(cells // 2):
            own[number, i] = paired(field[i], field[cells - 1 - i])
    for message in (low, high):
        for tap in range(3):
            message[PLANES, tap * cells : (tap + 1) * cells] = weight[tap]
        message[PLANES, 3 * cells : rows] = jnp.zeros((rows - 3 * cells, LANES), jnp.float32)


def spread_kernel(before, after, rotor, spread):
    own = rotor[...]
    rim = jnp.where(iota(own.shape, 1) < HALF, after[...], before[...])
    for k in range(spread.shape[0]):
        spread[k, 0:8] = own
        spread[k, 8:16] = rim


def corner_kernel(before, after, corner):
    strips = before.shape[0] - 24
    corner[0:strips] = before[0:strips]
    corner[strips : 2 * strips] = after[0:strips]
    left = iota((24, LANES), 1) < HALF
    corner[2 * strips : 2 * strips + 24] = jnp.where(left, after[strips:], before[strips:])


def basis_kernel(
    offset,
    weight,
    own,
    lower,
    upper,
    before,
    after,
    lower_rim,
    upper_rim,
    turned,
    p0,
    p1,
    p2,
    s0,
    s1,
    s2,
    sums,
    v0,
    v1,
    v2,
    diag,
    strip,
    taps,
    rot,
    mirror,
    line,
    face,
):
    cells = weight.shape[1]
    pairs = cells // 2
    last = HALO + pairs - 1
    total = turned.shape[0] * cells
    every = range(TILES + 2)
    place = lax.axis_index("radax")
    has_before, has_after = place > 0, place < lax.axis_size("radax") - 1
    lane = iota((8, LANES), 1)
    first_cell = lane % HALF == 0
    last_cell = lane % HALF == HALF - 1
    sign = jnp.where(lane < HALF, 1.0, -1.0)
    tenth = 0.1 * sign

    def walled(t, value):
        if t == 0:
            return jnp.where(has_before, value, 0.0)
        if t == TILES + 1:
            return jnp.where(has_after, value, 0.0)
        return value

    def seam(field):
        for t in every:
            field[last + 1, at(t)] = spin(field[last, at(t)], HALF)

    shift = 6.0 - CENTER
    for number, field in enumerate((v0, v1, v2, diag)):
        extra = shift if number == 3 else 0.0
        depth, start = DEPTHS[number], STARTS[number]
        for i in range(HALO - depth, HALO):
            block = paired(lower[start + i - HALO + depth], upper[start + HALO - 1 - i])
            field[i, BODY] = block + extra if number == 3 else block

        def fill(i, carry):
            block = own[number, i]
            field[HALO + i, BODY] = block + extra if number == 3 else block
            return carry

        lax.fori_loop(0, pairs, fill, 0, unroll=True)

    left = iota((STRIP, LANES), 1) < HALF
    size = STRIP * pairs
    for side, message in enumerate((before, after)):
        for i in range(HALO + pairs):
            pair = max(HALO - 1 - i, 0) if i else pairs - 1
            rows = slice(side * size + STRIP * pair, side * size + STRIP * pair + STRIP)
            if i >= HALO:
                strip[side, i] = message[STRIP * (i - HALO) : STRIP * (i - HALO) + STRIP]
            elif i:
                strip[side, i] = spin(jnp.where(left, upper_rim[rows], lower_rim[rows]), HALF)
            else:
                strip[side, i] = jnp.where(left, lower_rim[rows], upper_rim[rows])
    for number, field in enumerate((v0, v1, v2, diag)):
        reach, start = REACH[number], FROM[number]
        for i in range(HALO - DEPTHS[number], HALO + pairs):
            for side, t in ((0, 0), (1, TILES + 1)):
                value = walled(t, strip[side, i, start : start + reach])
                value = value + shift if number == 3 else value
                row = FRONT - reach if side == 0 else FRONT + LANES
                field[i, row : row + reach] = value
    for field in (v0, v1, v2):
        seam(field)

    wide = cells + 6
    rim_left = iota((cells, LANES), 1) < HALF
    for tap in range(3):
        k = tap * cells
        taps[0, tap, 0:3] = lower[PLANES, k + cells - 3 : k + cells]
        taps[0, tap, 3 : 3 + cells] = weight[tap]
        taps[0, tap, 3 + cells : wide] = upper[PLANES, k : k + 3]
        k += 2 * size
        taps[1, tap, 0:3] = lower_rim[k + cells - 3 : k + cells]
        k -= size
        taps[1, tap, 3 : 3 + cells] = jnp.where(
            rim_left, after[k : k + cells], before[k : k + cells]
        )
        k += size
        taps[1, tap, 3 + cells : wide] = upper_rim[k : k + 3]
    begin = lax.axis_index("azim") * cells - offset[0] - 4 + 2 * total
    for k in range(wide + 2):
        source = lax.rem(begin + k, total)
        block = source // cells
        row = lax.rem(source, cells)
        rot[0, k : k + 1] = turned[block, pl.ds(row, 1)]
        rot[1, k : k + 1] = turned[block, pl.ds(row + 8, 1)]
    for part in range(2):
        flux = jnp.zeros((wide, LANES), jnp.float32)
        for tap in range(3):
            flux += taps[part, tap, 0:wide] * rot[part, tap : tap + wide]
        mirror[2 : 2 + wide // 2] = flux[0 : wide // 2]
        for i in range(2, last + 1):
            mirror[HALF + i : HALF + i + 1] = flux[wide + 1 - i : wide + 2 - i]
        columns = mirror[...].T
        if part == 0:
            line[BODY] = columns
        else:
            line[FRONT + LANES : FRONT + LANES + 8] = columns[0:8]
            line[FRONT - 8 : FRONT] = columns[LANES - 8 : LANES]
    for i in range(2, last + 1):
        for t in every:
            face[i, at(t)] = spin(line[at(t)], -i)

    def radial(tile, inner):
        inward = jnp.where(first_cell, inner, spin(tile, 1))
        outward = jnp.where(last_cell, 0.0, spin(tile, -1))
        return inward, outward

    def advance(field, i, t, inner):
        x, lo, hi = field[i, at(t)], field[i - 1, at(t)], field[i + 1, at(t)]
        inward, outward = radial(x, inner)
        around = (field[i, at(t, -1)] + field[i, at(t, 1)]) + (inward + outward) + (lo + hi)
        wind = tenth * v0[i, at(t)]
        return walled(t, (0.4 * x + 0.1 * around) - wind * (hi - lo))

    def first_component(i, carry):
        for t in every:
            p0[i, at(t)] = advance(v0, i, t, 0.0)
        return carry

    def other_components(i, carry):
        for t in every:
            p1[i, at(t)] = advance(v1, i, t, face[i, at(t)])
            p2[i, at(t)] = advance(v2, i, t, 0.0)
        return carry

    def divergence(i, carry):
        for t in every:
            inward, outward = radial(p1[i, at(t)], face[i, at(t)])
            value = sign * (p0[i + 1, at(t)] - p0[i - 1, at(t)]) + (outward - inward)
            value = value + (p2[i, at(t, 1)] - p2[i, at(t, -1)])
            s0[i, at(t)] = walled(t, 0.5 * value)
        return carry

    def apply(field, i, t):
        x = field[i, at(t)]
        inward, outward = radial(x, 0.0)
        around = (field[i, at(t, -1)] + field[i, at(t, 1)]) + (inward + outward)
        around = around + (field[i - 1, at(t)] + field[i + 1, at(t)])
        return walled(t, diag[i, at(t)] * x - around)

    def second(i, carry):
        for t in every:
            s1[i, at(t)] = apply(s0, i, t)
        return carry

    def third(i, carry):
        for t in every:
            s2[i, at(t)] = apply(s1, i, t)
        return carry

    def products(i, carry):
        for t in range(1, TILES + 1):
            fourth = apply(s2, i, t)
            a, b, c = s0[i, at(t)], s1[i, at(t)], s2[i, at(t)]
            factors = ((a, a), (a, b), (b, b), (b, c), (c, c), (c, fourth))
            carry = tuple(s + x * y for s, (x, y) in zip(carry, factors))
        return carry

    lax.fori_loop(1, last + 1, first_component, 0, unroll=True)
    seam(p0)
    lax.fori_loop(2, last + 1, other_components, 0, unroll=True)
    lax.fori_loop(2, last + 1, divergence, 0, unroll=True)
    seam(s0)
    lax.fori_loop(3, last + 1, second, 0, unroll=True)
    seam(s1)
    lax.fori_loop(4, last + 1, third, 0, unroll=True)
    seam(s2)
    zero = jnp.zeros((8, LANES), jnp.float32)
    parts = lax.fori_loop(HALO, last + 1, products, (zero,) * 6, unroll=True)

    group = iota((1, LANES), 1) // 16
    packed = jnp.zeros((1, LANES), jnp.float32)
    for k, part in enumerate(parts):
        part = jnp.sum(part, axis=0, keepdims=True)
        for step in (64, 32, 16):
            part = part + pltpu.roll(part, step, 1)
        packed = jnp.where(group == k, part, packed)
    sums[...] = jnp.broadcast_to(packed[None], sums.shape)


def coefficients(nu):
    def product(x, y):
        total = 0.0
        for i, a in enumerate(x):
            for j, b in enumerate(y):
                total = total + a * b * nu[i + j]
        return total

    def energy(x):
        total = 0.0
        for i, a in enumerate(x):
            for j, b in enumerate(x):
                total = total + a * b * (nu[i + j + 1] + CENTER * nu[i + j])
        return total

    def image(x):
        out = [CENTER * a for a in x] + [0.0 * x[0]]
        return [out[0]] + [out[i + 1] + x[i] for i in range(len(x))]

    def length(norm, bottom):
        return jnp.clip(norm / bottom, 0.0624, 2.01)

    one = jnp.ones_like(nu[0])
    residual, direction, norm = [one], [one], nu[0]
    answer = [0.0 * one] * 3
    for step in range(3):
        alpha = length(norm, energy(direction))
        answer = [
            a + alpha * direction[i] if i < len(direction) else a for i, a in enumerate(answer)
        ]
        if step == 2:
            break
        moved = image(direction)
        residual = residual + [0.0 * one] * (len(moved) - len(residual))
        residual = [r - alpha * m for r, m in zip(residual, moved)]
        after = product(residual, residual)
        beta = after / norm
        padded = direction + [0.0 * one]
        direction = [r + beta * d for r, d in zip(residual, padded)]
        norm = after
    return answer


def project_kernel(sums, p0, p1, p2, s0, s1, s2, velocity, pressure, field, done):
    cells, rows = pressure.shape[0], pressure.shape[1]
    pairs = cells // 2
    last = HALO + pairs - 1
    lane = iota((8, LANES), 1)
    first_cell = lane % HALF == 0
    last_cell = lane % HALF == HALF - 1
    half = jnp.where(lane < HALF, 0.5, -0.5)
    total = jnp.sum(sums[...], axis=0)
    group = iota((1, LANES), 1) // 16
    nu = [jnp.sum(jnp.where(group == k, total, 0.0), axis=1, keepdims=True) for k in range(6)]
    c0, c1, c2 = coefficients(nu)

    def combine(i, carry):
        for t in range(TILES + 2):
            value = c0 * s0[i, at(t)] + c1 * s1[i, at(t)] + c2 * s2[i, at(t)]
            field[i, at(t)] = value
        return carry

    lax.fori_loop(HALO - 1, last + 1, combine, 0, unroll=True)
    for t in range(1, TILES + 1):
        field[last + 1, at(t)] = spin(field[last, at(t)], HALF)

    def gradient(i, carry):
        for t in range(1, TILES + 1):
            x = field[i, at(t)]
            inward = jnp.where(first_cell, 0.0, spin(x, 1))
            outward = jnp.where(last_cell, 0.0, spin(x, -1))
            around = half * (field[i + 1, at(t)] - field[i - 1, at(t)])
            along = 0.5 * (field[i, at(t, 1)] - field[i, at(t, -1)])
            own = slice(8 * t - 8, 8 * t)
            done[0, own] = p0[i, at(t)] - around
            done[1, own] = p1[i, at(t)] - 0.5 * (outward - inward)
            done[2, own] = p2[i, at(t)] - along
        for k in range(3):
            planes = done[k].T
            velocity[k, i - HALO] = planes[0:rows]
            velocity[k, last + pairs - i] = planes[rows:]
        planes = field[i, BODY].T
        pressure[i - HALO] = planes[0:rows]
        pressure[last + pairs - i] = planes[rows:]
        return carry

    lax.fori_loop(HALO, last + 1, gradient, 0, unroll=True)


def call(kernel, shapes, operands, scratch=(), spaces=None, sems=0, limit=VMEM_LIMIT):
    spec = lambda space: pl.BlockSpec(memory_space=space)
    spaces = spaces or [pltpu.VMEM] * len(operands)
    buffers = [pltpu.VMEM(s, jnp.float32) for s in scratch]
    if sems:
        buffers.append(pltpu.SemaphoreType.DMA((sems,)))
    return pl.pallas_call(
        kernel,
        out_shape=[jax.ShapeDtypeStruct(s, jnp.float32) for s in shapes],
        in_specs=[spec(space) for space in spaces],
        out_specs=[spec(pltpu.VMEM)] * len(shapes),
        scratch_shapes=buffers,
        compiler_params=pltpu.CompilerParams(vmem_limit_bytes=limit),
    )(*operands)


def swap(low, high, axis):
    count = lax.axis_size(axis)
    up = [(i, (i + 1) % count) for i in range(count)]
    down = [(j, i) for i, j in up]
    return lax.ppermute(high, axis, up), lax.ppermute(low, axis, down)


def per_device(velocity, rotor_flux, correlation_weight, damping, offset):
    cells, rows = damping.shape[0], damping.shape[1]
    azim = lax.axis_size("azim")
    devices = azim * lax.axis_size("radax")
    plane = (rows, LANES)
    block = (LANES, LANES)
    pairs = cells // 2
    rotor_before, rotor_after = swap(rotor_flux, rotor_flux, "radax")
    strips = (STRIP * pairs + 3 * cells, LANES)
    to_left, to_right = call(
        edge_kernel,
        [strips, strips],
        (velocity, damping, correlation_weight),
        scratch=[(3, cells) + plane, (cells,) + plane, (3, cells, LANES), block],
        spaces=[pl.ANY] * 3,
        sems=5,
        limit=WHOLE_VMEM,
    )
    before, after = swap(to_left, to_right, "radax")
    message = (PLANES + 1,) + plane
    low, high, own = call(
        plane_kernel,
        [message, message, (4, pairs) + block],
        (velocity, damping, correlation_weight, to_left),
        spaces=[pltpu.VMEM] * 3 + [pl.ANY],
    )
    lower, upper = swap(low, high, "azim")
    (spread,) = call(
        spread_kernel, [(azim, 16, LANES)], (rotor_before, rotor_after, rotor_flux)
    )
    turned = lax.all_to_all(spread, "azim", 0, 0, tiled=True)
    (corner,) = call(
        corner_kernel, [(2 * STRIP * pairs + 3 * cells, LANES)], (before, after)
    )
    lower_rim, upper_rim = swap(corner, corner, "azim")
    field = (HALO + pairs + 1, TALL, LANES)
    *fields, sums = call(
        basis_kernel,
        [field] * 6 + [(devices, 1, LANES)],
        (
            offset,
            correlation_weight,
            own,
            lower,
            upper,
            before,
            after,
            lower_rim,
            upper_rim,
            turned,
        ),
        scratch=[field] * 4
        + [
            (2, HALO + pairs, STRIP, LANES),
            (2, 3, cells + 8, LANES),
            (2, cells + 8, LANES),
            block,
            (TALL, LANES),
            field,
        ],
        spaces=[pltpu.SMEM] + [pltpu.VMEM] * 9,
    )
    sums = lax.all_to_all(sums, ("azim", "radax"), 0, 0, tiled=True)
    return call(
        project_kernel,
        [(3, cells) + plane, (cells,) + plane],
        (sums, *fields),
        scratch=[field, (3,) + block],
    )


def solution(mesh):
    in_specs = (
        P(None, "azim", None, "radax"),
        P("azim", "radax"),
        P(None, "azim", "radax"),
        P("azim", None, "radax"),
        P(),
    )
    out_specs = (P(None, "azim", None, "radax"), P("azim", None, "radax"))

    def run(*args):
        return tuple(per_device(*args))

    return jax.shard_map(run, mesh=mesh, in_specs=in_specs, out_specs=out_specs, check_vma=False)
```

```python
import jax
import jax.numpy as jnp
from jax import lax
from jax.experimental import pallas as pl
from jax.experimental.pallas import tpu as pltpu
from jax.sharding import PartitionSpec as P


CENTER = 8.0
HALO = 5
LANES = 128
HALF = 64
FRONT = 16
TALL = LANES + 2 * FRONT
TILES = LANES // 8
VMEM_LIMIT = 32 * 1024 * 1024
DEPTHS = (5, 4, 4, 2)
STARTS = (0, 5, 9, 13)
PLANES = 15
REACH = (4, 4, 5, 2)
FROM = (0, 4, 8, 13)
STRIP = 16
RIM = 16
BODY = slice(FRONT, FRONT + LANES)


def iota(shape, dim):
    return lax.broadcasted_iota(jnp.int32, shape, dim)


def spin(tile, steps):
    return pltpu.roll(tile, steps % LANES, 1) if steps % LANES else tile


def at(t, shift=0):
    start = FRONT - 8 + 8 * t + shift
    return slice(start, start + 8)


def paired(first, second):
    return jnp.concatenate([first, second], axis=0).T


def edge_kernel(
    velocity,
    damping,
    weight,
    rotor,
    to_left,
    to_right,
    low,
    high,
    own,
    vel,
    damp,
    wt,
    rt,
    sems,
):
    cells, rows = damping.shape[0], damping.shape[1]
    pairs = cells // 2
    copies = [pltpu.make_async_copy(velocity.at[k], vel.at[k], sems.at[k]) for k in range(3)]
    copies += [pltpu.make_async_copy(damping, damp, sems.at[3])]
    copies += [pltpu.make_async_copy(weight, wt, sems.at[4])]
    copies += [pltpu.make_async_copy(rotor, rt, sems.at[5])]
    for copy in copies:
        copy.start()
    fields = [vel.at[0], vel.at[1], vel.at[2], damp]
    for number, field in enumerate(fields):
        copies[number].wait()
        reach, start = REACH[number], FROM[number]
        for i in range(pairs):
            base = STRIP * i + start
            own[number, i] = paired(field[i], field[cells - 1 - i])
            to_left[base : base + reach] = own[number, i, 0:reach]
            to_right[base : base + reach] = own[number, i, LANES - reach : LANES]
        depth, start = DEPTHS[number], STARTS[number]
        low[start : start + depth] = field[0:depth]
        high[start : start + depth] = field[cells - depth : cells]
    for message in (to_left, to_right):
        for i in range(pairs):
            row = STRIP * i + STRIP - 1
            message[row : row + 1] = jnp.zeros((1, LANES), jnp.float32)
    for copy in copies[4:]:
        copy.wait()
    base = STRIP * pairs
    for tap in range(3):
        rows = slice(tap * cells, (tap + 1) * cells)
        low[PLANES, rows] = wt[tap]
        high[PLANES, rows] = wt[tap]
        rows = slice(base + tap * cells, base + (tap + 1) * cells)
        to_left[rows] = wt[tap]
        to_right[rows] = wt[tap]
    rows = slice(base + 3 * cells, base + 4 * cells)
    to_left[rows] = rt[...]
    to_right[rows] = rt[...]


def corner_kernel(before, after, sent, low_in, high_in, low, high, spread, ready, sem):
    rows, cells = low.shape[1], ready.shape[2] // LANES - 1
    strips = before.shape[0] - 4 * cells
    lines = strips + 3 * cells
    left = iota((3 * cells, LANES), 1) < HALF
    rims = jnp.where(left, after[strips:lines], before[strips:lines])
    own = sent[lines : lines + cells]
    rim = jnp.where(left[0:cells], after[lines : lines + cells], before[lines : lines + cells])
    group = iota((1, LANES), 1) // RIM
    packed = jnp.zeros((1, LANES), jnp.float32)
    for r in range(cells):
        packed = jnp.where(group == r, spin(rim[r : r + 1], RIM // 2 + RIM * r), packed)
    for k in range(ready.shape[0]):
        for r in range(cells):
            ready[k, :, LANES * r : LANES * r + LANES] = own[r : r + 1]
        ready[k, :, LANES * cells :] = packed
    copy = pltpu.make_async_copy(ready, spread, sem.at[0])
    copy.start()
    for message, base in ((low, low_in), (high, high_in)):
        message[0:PLANES] = base[0:PLANES]
        message[PLANES, 0 : 3 * cells] = base[PLANES, 0 : 3 * cells]
        message[PLANES, 3 * cells : 6 * cells] = rims
        message[PLANES, 6 * cells : rows] = jnp.zeros((rows - 6 * cells, LANES), jnp.float32)
        message[PLANES + 1] = before[0:strips]
        message[PLANES + 2] = after[0:strips]
    copy.wait()


def basis_kernel(
    offset,
    own,
    mine,
    lower,
    upper,
    turned,
    p0,
    p1,
    p2,
    s0,
    s1,
    s2,
    sums,
    v0,
    v1,
    v2,
    diag,
    strip,
    taps,
    rot,
    mirror,
    line,
    face,
):
    pairs = own.shape[1]
    cells = 2 * pairs
    last = HALO + pairs - 1
    total = turned.shape[0] * cells
    every = range(TILES + 2)
    place = lax.axis_index("radax")
    has_before, has_after = place > 0, place < lax.axis_size("radax") - 1
    lane = iota((8, LANES), 1)
    first_cell = lane % HALF == 0
    last_cell = lane % HALF == HALF - 1
    sign = jnp.where(lane < HALF, 1.0, -1.0)
    tenth = 0.1 * sign

    def walled(t, value):
        if t == 0:
            return jnp.where(has_before, value, 0.0)
        if t == TILES + 1:
            return jnp.where(has_after, value, 0.0)
        return value

    def seam(field):
        for t in every:
            field[last + 1, at(t)] = spin(field[last, at(t)], HALF)

    shift = 6.0 - CENTER
    for number, field in enumerate((v0, v1, v2, diag)):
        extra = shift if number == 3 else 0.0
        depth, start = DEPTHS[number], STARTS[number]
        for i in range(HALO - depth, HALO):
            block = paired(lower[start + i - HALO + depth], upper[start + HALO - 1 - i])
            field[i, BODY] = block + extra if number == 3 else block

        def fill(i, carry):
            block = own[number, i]
            field[HALO + i, BODY] = block + extra if number == 3 else block
            return carry

        lax.fori_loop(0, pairs, fill, 0, unroll=True)

    left = iota((STRIP, LANES), 1) < HALF
    for side in range(2):
        for i in range(HALO + pairs):
            pair = i - HALO if i >= HALO else min(HALO - 1 - i, pairs - 1)
            rows = slice(STRIP * pair, STRIP * pair + STRIP)
            under, over = lower[PLANES + 1 + side, rows], upper[PLANES + 1 + side, rows]
            if i >= HALO:
                strip[side, i] = mine[PLANES + 1 + side, rows]
            elif i:
                strip[side, i] = spin(jnp.where(left, over, under), HALF)
            else:
                strip[side, i] = jnp.where(left, under, over)
    for number, field in enumerate((v0, v1, v2, diag)):
        reach, start = REACH[number], FROM[number]
        for i in range(HALO - DEPTHS[number], HALO + pairs):
            for side, t in ((0, 0), (1, TILES + 1)):
                value = walled(t, strip[side, i, start : start + reach])
                value = value + shift if number == 3 else value
                row = FRONT - reach if side == 0 else FRONT + LANES
                field[i, row : row + reach] = value
    for field in (v0, v1, v2):
        seam(field)

    wide = cells + 6
    for part in range(2):
        for tap in range(3):
            k = (3 * part + tap) * cells
            taps[part, tap, 0:3] = lower[PLANES, k + cells - 3 : k + cells]
            taps[part, tap, 3 : 3 + cells] = mine[PLANES, k : k + cells]
            taps[part, tap, 3 + cells : wide] = upper[PLANES, k : k + 3]
    begin = lax.axis_index("azim") * cells - offset[0] - 4 + 2 * total
    for k in range(wide + 2):
        source = lax.rem(begin + k, total)
        block = source // cells
        row = lax.rem(source, cells)
        rot[0, k : k + 1] = turned[block, :, pl.ds(pl.multiple_of(row * LANES, LANES), LANES)]
        packed = turned[block, :, LANES * cells :]
        rot[1, k : k + 1] = pltpu.roll(packed, 2 * LANES - RIM // 2 - RIM * row, 1)
    for part in range(2):
        flux = jnp.zeros((wide, LANES), jnp.float32)
        for tap in range(3):
            flux += taps[part, tap, 0:wide] * rot[part, tap : tap + wide]
        mirror[2 : 2 + wide // 2] = flux[0 : wide // 2]
        for i in range(2, last + 1):
            mirror[HALF + i : HALF + i + 1] = flux[wide + 1 - i : wide + 2 - i]
        columns = mirror[...].T
        if part == 0:
            line[BODY] = columns
        else:
            line[FRONT + LANES : FRONT + LANES + 8] = columns[0:8]
            line[FRONT - 8 : FRONT] = columns[LANES - 8 : LANES]
    for i in range(2, last + 1):
        for t in every:
            face[i, at(t)] = spin(line[at(t)], -i)

    def radial(tile, inner):
        inward = jnp.where(first_cell, inner, spin(tile, 1))
        outward = jnp.where(last_cell, 0.0, spin(tile, -1))
        return inward, outward

    def advance(field, i, t, inner):
        x, lo, hi = field[i, at(t)], field[i - 1, at(t)], field[i + 1, at(t)]
        inward, outward = radial(x, inner)
        around = (field[i, at(t, -1)] + field[i, at(t, 1)]) + (inward + outward) + (lo + hi)
        wind = tenth * v0[i, at(t)]
        return walled(t, (0.4 * x + 0.1 * around) - wind * (hi - lo))

    def first_component(i, carry):
        for t in every:
            p0[i, at(t)] = advance(v0, i, t, 0.0)
        return carry

    def other_components(i, carry):
        for t in every:
            p1[i, at(t)] = advance(v1, i, t, face[i, at(t)])
            p2[i, at(t)] = advance(v2, i, t, 0.0)
        return carry

    def divergence(i, carry):
        for t in every:
            inward, outward = radial(p1[i, at(t)], face[i, at(t)])
            value = sign * (p0[i + 1, at(t)] - p0[i - 1, at(t)]) + (outward - inward)
            value = value + (p2[i, at(t, 1)] - p2[i, at(t, -1)])
            s0[i, at(t)] = walled(t, 0.5 * value)
        return carry

    def apply(field, i, t):
        x = field[i, at(t)]
        inward, outward = radial(x, 0.0)
        around = (field[i, at(t, -1)] + field[i, at(t, 1)]) + (inward + outward)
        around = around + (field[i - 1, at(t)] + field[i + 1, at(t)])
        return walled(t, diag[i, at(t)] * x - around)

    def second(i, carry):
        for t in every:
            s1[i, at(t)] = apply(s0, i, t)
        return carry

    def third(i, carry):
        for t in every:
            s2[i, at(t)] = apply(s1, i, t)
        return carry

    def products(i, carry):
        for t in range(1, TILES + 1):
            fourth = apply(s2, i, t)
            a, b, c = s0[i, at(t)], s1[i, at(t)], s2[i, at(t)]
            factors = ((a, a), (a, b), (b, b), (b, c), (c, c), (c, fourth))
            carry = tuple(s + x * y for s, (x, y) in zip(carry, factors))
        return carry

    lax.fori_loop(1, last + 1, first_component, 0, unroll=True)
    seam(p0)
    lax.fori_loop(2, last + 1, other_components, 0, unroll=True)
    lax.fori_loop(2, last + 1, divergence, 0, unroll=True)
    seam(s0)
    lax.fori_loop(3, last + 1, second, 0, unroll=True)
    seam(s1)
    lax.fori_loop(4, last + 1, third, 0, unroll=True)
    seam(s2)
    zero = jnp.zeros((8, LANES), jnp.float32)
    parts = lax.fori_loop(HALO, last + 1, products, (zero,) * 6, unroll=True)

    group = iota((1, LANES), 1) // 16
    packed = jnp.zeros((1, LANES), jnp.float32)
    for k, part in enumerate(parts):
        part = jnp.sum(part, axis=0, keepdims=True)
        for step in (64, 32, 16):
            part = part + pltpu.roll(part, step, 1)
        packed = jnp.where(group == k, part, packed)
    sums[...] = jnp.broadcast_to(packed[None], sums.shape)


def coefficients(nu):
    def product(x, y):
        total = 0.0
        for i, a in enumerate(x):
            for j, b in enumerate(y):
                total = total + a * b * nu[i + j]
        return total

    def energy(x):
        total = 0.0
        for i, a in enumerate(x):
            for j, b in enumerate(x):
                total = total + a * b * (nu[i + j + 1] + CENTER * nu[i + j])
        return total

    def image(x):
        out = [CENTER * a for a in x] + [0.0 * x[0]]
        return [out[0]] + [out[i + 1] + x[i] for i in range(len(x))]

    def length(norm, bottom):
        return jnp.clip(norm / bottom, 0.0624, 2.01)

    one = jnp.ones_like(nu[0])
    residual, direction, norm = [one], [one], nu[0]
    answer = [0.0 * one] * 3
    for step in range(3):
        alpha = length(norm, energy(direction))
        answer = [
            a + alpha * direction[i] if i < len(direction) else a for i, a in enumerate(answer)
        ]
        if step == 2:
            break
        moved = image(direction)
        residual = residual + [0.0 * one] * (len(moved) - len(residual))
        residual = [r - alpha * m for r, m in zip(residual, moved)]
        after = product(residual, residual)
        beta = after / norm
        padded = direction + [0.0 * one]
        direction = [r + beta * d for r, d in zip(residual, padded)]
        norm = after
    return answer


def project_kernel(sums, p0, p1, p2, s0, s1, s2, velocity, pressure, field, done):
    cells, rows = pressure.shape[0], pressure.shape[1]
    pairs = cells // 2
    last = HALO + pairs - 1
    lane = iota((8, LANES), 1)
    first_cell = lane % HALF == 0
    last_cell = lane % HALF == HALF - 1
    half = jnp.where(lane < HALF, 0.5, -0.5)
    total = jnp.sum(sums[...], axis=0)
    group = iota((1, LANES), 1) // 16
    nu = [jnp.sum(jnp.where(group == k, total, 0.0), axis=1, keepdims=True) for k in range(6)]
    c0, c1, c2 = coefficients(nu)

    def combine(i, carry):
        for t in range(TILES + 2):
            value = c0 * s0[i, at(t)] + c1 * s1[i, at(t)] + c2 * s2[i, at(t)]
            field[i, at(t)] = value
        return carry

    lax.fori_loop(HALO - 1, last + 1, combine, 0, unroll=True)
    for t in range(1, TILES + 1):
        field[last + 1, at(t)] = spin(field[last, at(t)], HALF)

    def gradient(i, carry):
        for t in range(1, TILES + 1):
            x = field[i, at(t)]
            inward = jnp.where(first_cell, 0.0, spin(x, 1))
            outward = jnp.where(last_cell, 0.0, spin(x, -1))
            around = half * (field[i + 1, at(t)] - field[i - 1, at(t)])
            along = 0.5 * (field[i, at(t, 1)] - field[i, at(t, -1)])
            own = slice(8 * t - 8, 8 * t)
            done[0, own] = p0[i, at(t)] - around
            done[1, own] = p1[i, at(t)] - 0.5 * (outward - inward)
            done[2, own] = p2[i, at(t)] - along
        for k in range(3):
            planes = done[k].T
            velocity[k, i - HALO] = planes[0:rows]
            velocity[k, last + pairs - i] = planes[rows:]
        planes = field[i, BODY].T
        pressure[i - HALO] = planes[0:rows]
        pressure[last + pairs - i] = planes[rows:]
        return carry

    lax.fori_loop(HALO, last + 1, gradient, 0, unroll=True)


def call(
    kernel, shapes, operands, scratch=(), spaces=None, outs=None, sems=0
):
    spec = lambda space: pl.BlockSpec(memory_space=space)
    spaces = spaces or [pltpu.VMEM] * len(operands)
    outs = outs or [pltpu.VMEM] * len(shapes)
    operands = [
        pltpu.with_memory_space_constraint(x, pltpu.HBM) if space is pltpu.HBM else x
        for x, space in zip(operands, spaces)
    ]
    buffers = [pltpu.VMEM(s, jnp.float32) for s in scratch]
    if sems:
        buffers.append(pltpu.SemaphoreType.DMA((sems,)))
    return pl.pallas_call(
        kernel,
        out_shape=[
            space(s, jnp.float32) if space is pltpu.HBM else jax.ShapeDtypeStruct(s, jnp.float32)
            for s, space in zip(shapes, outs)
        ],
        in_specs=[spec(space) for space in spaces],
        out_specs=[spec(space) for space in outs],
        scratch_shapes=buffers,
        compiler_params=pltpu.CompilerParams(vmem_limit_bytes=VMEM_LIMIT),
    )(*operands)


def swap(low, high, axis):
    count = lax.axis_size(axis)
    up = [(i, (i + 1) % count) for i in range(count)]
    down = [(j, i) for i, j in up]
    return lax.ppermute(high, axis, up), lax.ppermute(low, axis, down)


def per_device(velocity, rotor_flux, correlation_weight, damping, offset):
    cells, rows = damping.shape[0], damping.shape[1]
    azim = lax.axis_size("azim")
    devices = azim * lax.axis_size("radax")
    plane = (rows, LANES)
    block = (LANES, LANES)
    pairs = cells // 2
    strips = (STRIP * pairs + 4 * cells, LANES)
    message = (PLANES + 3,) + plane
    to_left, to_right, low, high, own = call(
        edge_kernel,
        [strips, strips, message, message, (4, pairs) + block],
        (velocity, damping, correlation_weight, rotor_flux),
        scratch=[(3, cells) + plane, (cells,) + plane, (3, cells, LANES), (cells, LANES)],
        spaces=[pltpu.HBM] * 4,
        sems=6,
    )
    before, after = swap(to_left, to_right, "radax")
    low, high, spread = call(
        corner_kernel,
        [message, message, (azim, 1, LANES * (cells + 1))],
        (before, after, to_left, low, high),
        scratch=[(azim, 1, LANES * (cells + 1))],
        outs=[pltpu.VMEM, pltpu.VMEM, pltpu.HBM],
        sems=1,
    )
    lower, upper = swap(low, high, "azim")
    turned = lax.all_to_all(spread, "azim", 0, 0, tiled=True)
    field = (HALO + pairs + 1, TALL, LANES)
    *fields, sums = call(
        basis_kernel,
        [field] * 6 + [(devices, 1, LANES)],
        (offset, own, low, lower, upper, turned),
        scratch=[field] * 4
        + [
            (2, HALO + pairs, STRIP, LANES),
            (2, 3, cells + 8, LANES),
            (2, cells + 8, LANES),
            block,
            (TALL, LANES),
            field,
        ],
        spaces=[pltpu.SMEM] + [pltpu.VMEM] * 5,
    )
    sums = lax.all_to_all(sums, ("azim", "radax"), 0, 0, tiled=True)
    return call(
        project_kernel,
        [(3, cells) + plane, (cells,) + plane],
        (sums, *fields),
        scratch=[field, (3,) + block],
    )


def solution(mesh):
    in_specs = (
        P(None, "azim", None, "radax"),
        P("azim", "radax"),
        P(None, "azim", "radax"),
        P("azim", None, "radax"),
        P(),
    )
    out_specs = (P(None, "azim", None, "radax"), P("azim", None, "radax"))

    def run(*args):
        return tuple(per_device(*args))

    return jax.shard_map(run, mesh=mesh, in_specs=in_specs, out_specs=out_specs, check_vma=False)
```

```python
import jax
import jax.numpy as jnp
from jax import lax
from jax.experimental import pallas as pl
from jax.experimental.pallas import tpu as pltpu
from jax.sharding import PartitionSpec as P


CENTER = 8.0
HALO = 5
LANES = 128
HALF = 64
FRONT = 16
TALL = LANES + 2 * FRONT
TILES = LANES // 8
VMEM_LIMIT = 32 * 1024 * 1024
DEPTHS = (5, 4, 4, 2)
STARTS = (0, 5, 9, 13)
PLANES = 15
REACH = (4, 4, 5, 2)
FROM = (0, 4, 8, 13)
STRIP = 16
RIM = 16
BODY = slice(FRONT, FRONT + LANES)


def iota(shape, dim):
    return lax.broadcasted_iota(jnp.int32, shape, dim)


def spin(tile, steps):
    return pltpu.roll(tile, steps % LANES, 1) if steps % LANES else tile


def at(t, shift=0):
    start = FRONT - 8 + 8 * t + shift
    return slice(start, start + 8)


def paired(first, second):
    return jnp.concatenate([first, second], axis=0).T


def edge_kernel(
    velocity,
    damping,
    weight,
    rotor,
    beside_near,
    beside_far,
    near,
    far,
    own,
    vel,
    damp,
    wt,
    rt,
    sems,
):
    cells, rows = damping.shape[0], damping.shape[1]
    pairs = cells // 2
    even = lax.rem(lax.axis_index("azim"), 2) == 0
    even_axial = lax.rem(lax.axis_index("radax"), 2) == 0
    copies = [pltpu.make_async_copy(velocity.at[k], vel.at[k], sems.at[k]) for k in range(3)]
    copies += [pltpu.make_async_copy(damping, damp, sems.at[3])]
    copies += [pltpu.make_async_copy(weight, wt, sems.at[4])]
    copies += [pltpu.make_async_copy(rotor, rt, sems.at[5])]
    for copy in copies:
        copy.start()
    fields = [vel.at[0], vel.at[1], vel.at[2], damp]
    for number, field in enumerate(fields):
        copies[number].wait()
        reach, start = REACH[number], FROM[number]
        for i in range(pairs):
            base = STRIP * i + start
            own[number, i] = paired(field[i], field[cells - 1 - i])
            first, final = own[number, i, 0:reach], own[number, i, LANES - reach : LANES]
            beside_near[base : base + reach] = jnp.where(even_axial, final, first)
            beside_far[base : base + reach] = jnp.where(even_axial, first, final)
        depth, start = DEPTHS[number], STARTS[number]
        near[start : start + depth] = field[pl.ds(jnp.where(even, cells - depth, 0), depth)]
        far[start : start + depth] = field[pl.ds(jnp.where(even, 0, cells - depth), depth)]
    for message in (beside_near, beside_far):
        for i in range(pairs):
            row = STRIP * i + STRIP - 1
            message[row : row + 1] = jnp.zeros((1, LANES), jnp.float32)
    for copy in copies[4:]:
        copy.wait()
    base = STRIP * pairs
    for tap in range(3):
        rows = slice(tap * cells, (tap + 1) * cells)
        near[PLANES, rows] = wt[tap]
        far[PLANES, rows] = wt[tap]
        rows = slice(base + tap * cells, base + (tap + 1) * cells)
        beside_near[rows] = wt[tap]
        beside_far[rows] = wt[tap]
    rows = slice(base + 3 * cells, base + 4 * cells)
    beside_near[rows] = rt[...]
    beside_far[rows] = rt[...]


def corner_kernel(
    from_near, from_far, sent, near_in, far_in, near, far, spread, both, ready, sem
):
    odd = lax.rem(lax.axis_index("radax"), 2)
    both[1 - odd] = from_near[...]
    both[odd] = from_far[...]
    before, after = both.at[0], both.at[1]
    rows, cells = near.shape[1], ready.shape[2] // LANES - 1
    strips = before.shape[0] - 4 * cells
    lines = strips + 3 * cells
    left = iota((3 * cells, LANES), 1) < HALF
    rims = jnp.where(left, after[strips:lines], before[strips:lines])
    own = sent[lines : lines + cells]
    rim = jnp.where(left[0:cells], after[lines : lines + cells], before[lines : lines + cells])
    group = iota((1, LANES), 1) // RIM
    packed = jnp.zeros((1, LANES), jnp.float32)
    for r in range(cells):
        packed = jnp.where(group == r, spin(rim[r : r + 1], RIM // 2 + RIM * r), packed)
    for k in range(ready.shape[0]):
        for r in range(cells):
            ready[k, :, LANES * r : LANES * r + LANES] = own[r : r + 1]
        ready[k, :, LANES * cells :] = packed
    copy = pltpu.make_async_copy(ready, spread, sem.at[0])
    copy.start()
    for message, base in ((near, near_in), (far, far_in)):
        message[0:PLANES] = base[0:PLANES]
        message[PLANES, 0 : 3 * cells] = base[PLANES, 0 : 3 * cells]
        message[PLANES, 3 * cells : 6 * cells] = rims
        message[PLANES, 6 * cells : rows] = jnp.zeros((rows - 6 * cells, LANES), jnp.float32)
        message[PLANES + 1] = before[0:strips]
        message[PLANES + 2] = after[0:strips]
    copy.wait()


def basis_kernel(
    offset,
    own,
    mine,
    near,
    far,
    turned,
    p0,
    p1,
    p2,
    s0,
    s1,
    s2,
    sums,
    v0,
    v1,
    v2,
    diag,
    strip,
    taps,
    rot,
    mirror,
    line,
    face,
    halves,
):
    odd = lax.rem(lax.axis_index("azim"), 2)
    halves[1 - odd] = near[...]
    halves[odd] = far[...]
    lower, upper = halves.at[0], halves.at[1]
    pairs = own.shape[1]
    cells = 2 * pairs
    last = HALO + pairs - 1
    total = turned.shape[0] * cells
    every = range(TILES + 2)
    place = lax.axis_index("radax")
    has_before, has_after = place > 0, place < lax.axis_size("radax") - 1
    lane = iota((8, LANES), 1)
    first_cell = lane % HALF == 0
    last_cell = lane % HALF == HALF - 1
    sign = jnp.where(lane < HALF, 1.0, -1.0)
    tenth = 0.1 * sign

    def walled(t, value):
        if t == 0:
            return jnp.where(has_before, value, 0.0)
        if t == TILES + 1:
            return jnp.where(has_after, value, 0.0)
        return value

    def seam(field):
        for t in every:
            field[last + 1, at(t)] = spin(field[last, at(t)], HALF)

    shift = 6.0 - CENTER
    for number, field in enumerate((v0, v1, v2, diag)):
        extra = shift if number == 3 else 0.0
        depth, start = DEPTHS[number], STARTS[number]
        for i in range(HALO - depth, HALO):
            block = paired(lower[start + i - HALO + depth], upper[start + HALO - 1 - i])
            field[i, BODY] = block + extra if number == 3 else block

        def fill(i, carry):
            block = own[number, i]
            field[HALO + i, BODY] = block + extra if number == 3 else block
            return carry

        lax.fori_loop(0, pairs, fill, 0, unroll=True)

    left = iota((STRIP, LANES), 1) < HALF
    for side in range(2):
        for i in range(HALO + pairs):
            pair = i - HALO if i >= HALO else min(HALO - 1 - i, pairs - 1)
            rows = slice(STRIP * pair, STRIP * pair + STRIP)
            under, over = lower[PLANES + 1 + side, rows], upper[PLANES + 1 + side, rows]
            if i >= HALO:
                strip[side, i] = mine[PLANES + 1 + side, rows]
            elif i:
                strip[side, i] = spin(jnp.where(left, over, under), HALF)
            else:
                strip[side, i] = jnp.where(left, under, over)
    for number, field in enumerate((v0, v1, v2, diag)):
        reach, start = REACH[number], FROM[number]
        for i in range(HALO - DEPTHS[number], HALO + pairs):
            for side, t in ((0, 0), (1, TILES + 1)):
                value = walled(t, strip[side, i, start : start + reach])
                value = value + shift if number == 3 else value
                row = FRONT - reach if side == 0 else FRONT + LANES
                field[i, row : row + reach] = value
    for field in (v0, v1, v2):
        seam(field)

    wide = cells + 6
    for part in range(2):
        for tap in range(3):
            k = (3 * part + tap) * cells
            taps[part, tap, 0:3] = lower[PLANES, k + cells - 3 : k + cells]
            taps[part, tap, 3 : 3 + cells] = mine[PLANES, k : k + cells]
            taps[part, tap, 3 + cells : wide] = upper[PLANES, k : k + 3]
    begin = lax.axis_index("azim") * cells - offset[0] - 4 + 2 * total
    for k in range(wide + 2):
        source = lax.rem(begin + k, total)
        block = source // cells
        row = lax.rem(source, cells)
        rot[0, k : k + 1] = turned[block, :, pl.ds(pl.multiple_of(row * LANES, LANES), LANES)]
        packed = turned[block, :, LANES * cells :]
        rot[1, k : k + 1] = pltpu.roll(packed, 2 * LANES - RIM // 2 - RIM * row, 1)
    for part in range(2):
        flux = jnp.zeros((wide, LANES), jnp.float32)
        for tap in range(3):
            flux += taps[part, tap, 0:wide] * rot[part, tap : tap + wide]
        mirror[2 : 2 + wide // 2] = flux[0 : wide // 2]
        for i in range(2, last + 1):
            mirror[HALF + i : HALF + i + 1] = flux[wide + 1 - i : wide + 2 - i]
        columns = mirror[...].T
        if part == 0:
            line[BODY] = columns
        else:
            line[FRONT + LANES : FRONT + LANES + 8] = columns[0:8]
            line[FRONT - 8 : FRONT] = columns[LANES - 8 : LANES]
    for i in range(2, last + 1):
        for t in every:
            face[i, at(t)] = spin(line[at(t)], -i)

    def radial(tile, inner):
        inward = jnp.where(first_cell, inner, spin(tile, 1))
        outward = jnp.where(last_cell, 0.0, spin(tile, -1))
        return inward, outward

    def advance(field, i, t, inner):
        x, lo, hi = field[i, at(t)], field[i - 1, at(t)], field[i + 1, at(t)]
        inward, outward = radial(x, inner)
        around = (field[i, at(t, -1)] + field[i, at(t, 1)]) + (inward + outward) + (lo + hi)
        wind = tenth * v0[i, at(t)]
        return walled(t, (0.4 * x + 0.1 * around) - wind * (hi - lo))

    def first_component(i, carry):
        for t in every:
            p0[i, at(t)] = advance(v0, i, t, 0.0)
        return carry

    def other_components(i, carry):
        for t in every:
            p1[i, at(t)] = advance(v1, i, t, face[i, at(t)])
            p2[i, at(t)] = advance(v2, i, t, 0.0)
        return carry

    def divergence(i, carry):
        for t in every:
            inward, outward = radial(p1[i, at(t)], face[i, at(t)])
            value = sign * (p0[i + 1, at(t)] - p0[i - 1, at(t)]) + (outward - inward)
            value = value + (p2[i, at(t, 1)] - p2[i, at(t, -1)])
            s0[i, at(t)] = walled(t, 0.5 * value)
        return carry

    def apply(field, i, t):
        x = field[i, at(t)]
        inward, outward = radial(x, 0.0)
        around = (field[i, at(t, -1)] + field[i, at(t, 1)]) + (inward + outward)
        around = around + (field[i - 1, at(t)] + field[i + 1, at(t)])
        return walled(t, diag[i, at(t)] * x - around)

    def second(i, carry):
        for t in every:
            s1[i, at(t)] = apply(s0, i, t)
        return carry

    def third(i, carry):
        for t in every:
            s2[i, at(t)] = apply(s1, i, t)
        return carry

    def products(i, carry):
        for t in range(1, TILES + 1):
            fourth = apply(s2, i, t)
            a, b, c = s0[i, at(t)], s1[i, at(t)], s2[i, at(t)]
            factors = ((a, a), (a, b), (b, b), (b, c), (c, c), (c, fourth))
            carry = tuple(s + x * y for s, (x, y) in zip(carry, factors))
        return carry

    lax.fori_loop(1, last + 1, first_component, 0, unroll=True)
    seam(p0)
    lax.fori_loop(2, last + 1, other_components, 0, unroll=True)
    lax.fori_loop(2, last + 1, divergence, 0, unroll=True)
    seam(s0)
    lax.fori_loop(3, last + 1, second, 0, unroll=True)
    seam(s1)
    lax.fori_loop(4, last + 1, third, 0, unroll=True)
    seam(s2)
    zero = jnp.zeros((8, LANES), jnp.float32)
    parts = lax.fori_loop(HALO, last + 1, products, (zero,) * 6, unroll=True)

    group = iota((1, LANES), 1) // 16
    packed = jnp.zeros((1, LANES), jnp.float32)
    for k, part in enumerate(parts):
        part = jnp.sum(part, axis=0, keepdims=True)
        for step in (64, 32, 16):
            part = part + pltpu.roll(part, step, 1)
        packed = jnp.where(group == k, part, packed)
    sums[...] = jnp.broadcast_to(packed[None], sums.shape)


def coefficients(nu):
    def product(x, y):
        total = 0.0
        for i, a in enumerate(x):
            for j, b in enumerate(y):
                total = total + a * b * nu[i + j]
        return total

    def energy(x):
        total = 0.0
        for i, a in enumerate(x):
            for j, b in enumerate(x):
                total = total + a * b * (nu[i + j + 1] + CENTER * nu[i + j])
        return total

    def image(x):
        out = [CENTER * a for a in x] + [0.0 * x[0]]
        return [out[0]] + [out[i + 1] + x[i] for i in range(len(x))]

    def length(norm, bottom):
        return jnp.clip(norm / bottom, 0.0624, 2.01)

    one = jnp.ones_like(nu[0])
    residual, direction, norm = [one], [one], nu[0]
    answer = [0.0 * one] * 3
    for step in range(3):
        alpha = length(norm, energy(direction))
        answer = [
            a + alpha * direction[i] if i < len(direction) else a for i, a in enumerate(answer)
        ]
        if step == 2:
            break
        moved = image(direction)
        residual = residual + [0.0 * one] * (len(moved) - len(residual))
        residual = [r - alpha * m for r, m in zip(residual, moved)]
        after = product(residual, residual)
        beta = after / norm
        padded = direction + [0.0 * one]
        direction = [r + beta * d for r, d in zip(residual, padded)]
        norm = after
    return answer


def project_kernel(sums, p0, p1, p2, s0, s1, s2, velocity, pressure, field, done):
    cells, rows = pressure.shape[0], pressure.shape[1]
    pairs = cells // 2
    last = HALO + pairs - 1
    lane = iota((8, LANES), 1)
    first_cell = lane % HALF == 0
    last_cell = lane % HALF == HALF - 1
    half = jnp.where(lane < HALF, 0.5, -0.5)
    total = jnp.sum(sums[...], axis=0)
    group = iota((1, LANES), 1) // 16
    nu = [jnp.sum(jnp.where(group == k, total, 0.0), axis=1, keepdims=True) for k in range(6)]
    c0, c1, c2 = coefficients(nu)

    def combine(i, carry):
        for t in range(TILES + 2):
            value = c0 * s0[i, at(t)] + c1 * s1[i, at(t)] + c2 * s2[i, at(t)]
            field[i, at(t)] = value
        return carry

    lax.fori_loop(HALO - 1, last + 1, combine, 0, unroll=True)
    for t in range(1, TILES + 1):
        field[last + 1, at(t)] = spin(field[last, at(t)], HALF)

    def gradient(i, carry):
        for t in range(1, TILES + 1):
            x = field[i, at(t)]
            inward = jnp.where(first_cell, 0.0, spin(x, 1))
            outward = jnp.where(last_cell, 0.0, spin(x, -1))
            around = half * (field[i + 1, at(t)] - field[i - 1, at(t)])
            along = 0.5 * (field[i, at(t, 1)] - field[i, at(t, -1)])
            own = slice(8 * t - 8, 8 * t)
            done[0, own] = p0[i, at(t)] - around
            done[1, own] = p1[i, at(t)] - 0.5 * (outward - inward)
            done[2, own] = p2[i, at(t)] - along
        for k in range(3):
            planes = done[k].T
            velocity[k, i - HALO] = planes[0:rows]
            velocity[k, last + pairs - i] = planes[rows:]
        planes = field[i, BODY].T
        pressure[i - HALO] = planes[0:rows]
        pressure[last + pairs - i] = planes[rows:]
        return carry

    lax.fori_loop(HALO, last + 1, gradient, 0, unroll=True)


def call(
    kernel, shapes, operands, scratch=(), spaces=None, outs=None, sems=0
):
    spec = lambda space: pl.BlockSpec(memory_space=space)
    spaces = spaces or [pltpu.VMEM] * len(operands)
    outs = outs or [pltpu.VMEM] * len(shapes)
    operands = [
        pltpu.with_memory_space_constraint(x, pltpu.HBM) if space is pltpu.HBM else x
        for x, space in zip(operands, spaces)
    ]
    buffers = [pltpu.VMEM(s, jnp.float32) for s in scratch]
    if sems:
        buffers.append(pltpu.SemaphoreType.DMA((sems,)))
    return pl.pallas_call(
        kernel,
        out_shape=[
            space(s, jnp.float32) if space is pltpu.HBM else jax.ShapeDtypeStruct(s, jnp.float32)
            for s, space in zip(shapes, outs)
        ],
        in_specs=[spec(space) for space in spaces],
        out_specs=[spec(space) for space in outs],
        scratch_shapes=buffers,
        compiler_params=pltpu.CompilerParams(vmem_limit_bytes=VMEM_LIMIT),
    )(*operands)


def trade(near, far, axis):
    count = lax.axis_size(axis)
    first = [(i, i ^ 1) for i in range(count)]
    second = [(i, (i + 2 * (i % 2) - 1) % count) for i in range(count)]
    return lax.ppermute(near, axis, first), lax.ppermute(far, axis, second)


def per_device(velocity, rotor_flux, correlation_weight, damping, offset):
    cells, rows = damping.shape[0], damping.shape[1]
    azim = lax.axis_size("azim")
    devices = azim * lax.axis_size("radax")
    plane = (rows, LANES)
    block = (LANES, LANES)
    pairs = cells // 2
    strips = (STRIP * pairs + 4 * cells, LANES)
    message = (PLANES + 3,) + plane
    beside_near, beside_far, near, far, own = call(
        edge_kernel,
        [strips, strips, message, message, (4, pairs) + block],
        (velocity, damping, correlation_weight, rotor_flux),
        scratch=[(3, cells) + plane, (cells,) + plane, (3, cells, LANES), (cells, LANES)],
        spaces=[pltpu.HBM] * 4,
        sems=6,
    )
    from_near, from_far = trade(beside_near, beside_far, "radax")
    near, far, spread = call(
        corner_kernel,
        [message, message, (azim, 1, LANES * (cells + 1))],
        (from_near, from_far, beside_near, near, far),
        scratch=[(2,) + strips, (azim, 1, LANES * (cells + 1))],
        outs=[pltpu.VMEM, pltpu.VMEM, pltpu.HBM],
        sems=1,
    )
    from_near, from_far = trade(near, far, "azim")
    turned = lax.all_to_all(spread, "azim", 0, 0, tiled=True)
    field = (HALO + pairs + 1, TALL, LANES)
    *fields, sums = call(
        basis_kernel,
        [field] * 6 + [(devices, 1, LANES)],
        (offset, own, near, from_near, from_far, turned),
        scratch=[field] * 4
        + [
            (2, HALO + pairs, STRIP, LANES),
            (2, 3, cells + 8, LANES),
            (2, cells + 8, LANES),
            block,
            (TALL, LANES),
            field,
            (2,) + message,
        ],
        spaces=[pltpu.SMEM] + [pltpu.VMEM] * 5,
    )
    sums = lax.all_to_all(sums, ("azim", "radax"), 0, 0, tiled=True)
    return call(
        project_kernel,
        [(3, cells) + plane, (cells,) + plane],
        (sums, *fields),
        scratch=[field, (3,) + block],
    )


def solution(mesh):
    in_specs = (
        P(None, "azim", None, "radax"),
        P("azim", "radax"),
        P(None, "azim", "radax"),
        P("azim", None, "radax"),
        P(),
    )
    out_specs = (P(None, "azim", None, "radax"), P("azim", None, "radax"))

    def run(*args):
        return tuple(per_device(*args))

    return jax.shard_map(run, mesh=mesh, in_specs=in_specs, out_specs=out_specs, check_vma=False)
```

```python
import jax
import jax.numpy as jnp
from jax import lax
from jax.experimental import pallas as pl
from jax.experimental.pallas import tpu as pltpu
from jax.sharding import PartitionSpec as P


CENTER = 8.0
HALO = 5
LANES = 128
HALF = 64
FRONT = 16
TALL = LANES + 2 * FRONT
TILES = LANES // 8
VMEM_LIMIT = 32 * 1024 * 1024
DEPTHS = (5, 4, 4, 2)
STARTS = (0, 5, 9, 13)
PLANES = 15
REACH = (4, 4, 5, 2)
LAG = (0, 1, 0, 3)
STRIP = 16
RIM = 8
BODY = slice(FRONT, FRONT + LANES)


def strips(pairs):
    table, row = {}, 0
    for i in range(HALO + pairs):
        for number in range(4):
            reach = max(min(i - LAG[number], REACH[number]), 0)
            if reach:
                table[number, i] = (row, reach)
            row += reach
    return table, row + -row % 8


def iota(shape, dim):
    return lax.broadcasted_iota(jnp.int32, shape, dim)


def spin(tile, steps):
    return pltpu.roll(tile, steps % LANES, 1) if steps % LANES else tile


def at(t, shift=0):
    start = FRONT - 8 + 8 * t + shift
    return slice(start, start + 8)


def paired(first, second):
    return jnp.concatenate([first, second], axis=0).T


def plane_kernel(
    velocity, damping, weight, rotor, near, far, spread, vel, damp, lines, ready, sems
):
    cells, rows = damping.shape[0], damping.shape[1]
    even = lax.rem(lax.axis_index("azim"), 2) == 0
    first = pltpu.make_async_copy(rotor, lines, sems.at[0])
    first.start()
    copies = []

    def copy(source, target):
        copies.append(pltpu.make_async_copy(source, target, sems.at[1 + len(copies)]))
        copies[-1].start()

    fields = [velocity.at[0], velocity.at[1], velocity.at[2], damping]
    for field, depth, start in zip(fields, DEPTHS, STARTS):
        target = slice(start, start + depth)
        copy(field.at[pl.ds(jnp.where(even, cells - depth, 0), depth)], near.at[target])
        copy(field.at[pl.ds(jnp.where(even, 0, cells - depth), depth)], far.at[target])
    for tap in range(3):
        target = slice(tap * cells, (tap + 1) * cells)
        copy(weight.at[tap], near.at[PLANES, target])
        copy(weight.at[tap], far.at[PLANES, target])
    copy(velocity, vel)
    copy(damping, damp)
    for message in (near, far):
        message[PLANES, 3 * cells : rows] = jnp.zeros((rows - 3 * cells, LANES), jnp.float32)
    first.wait()
    ready[...] = jnp.broadcast_to(lines[...][None], ready.shape)
    copy(ready, spread)
    for each in copies:
        each.wait()


def gather_kernel(
    offset,
    velocity,
    damping,
    mine,
    near,
    far,
    turned,
    beside_near,
    beside_far,
    blocks,
    taps,
    rot,
    halves,
):
    cells = damping.shape[0]
    pairs = cells // 2
    odd = lax.rem(lax.axis_index("azim"), 2)
    even_axial = lax.rem(lax.axis_index("radax"), 2) == 0
    halves[1 - odd] = near[...]
    halves[odd] = far[...]
    lower, upper = halves.at[0], halves.at[1]

    total = turned.shape[0] * cells
    begin = lax.axis_index("azim") * cells - offset[0] - 4 + 2 * total
    for k in range(cells + 8):
        source = lax.rem(begin + k, total)
        rot[k : k + 1] = turned[source // cells, pl.ds(lax.rem(source, cells), 1)]
    wide = cells + 6
    for tap in range(3):
        k = tap * cells
        taps[tap, 0:3] = lower[PLANES, k + cells - 3 : k + cells]
        taps[tap, 3 : 3 + cells] = mine[PLANES, k : k + cells]
        taps[tap, 3 + cells : wide] = upper[PLANES, k : k + 3]
        taps[tap, wide : wide + 2] = jnp.zeros((2, LANES), jnp.float32)

    table, count = strips(pairs)
    group = iota((STRIP, LANES), 1) // RIM
    firsts = finals = jnp.zeros((STRIP, LANES), jnp.float32)
    for k, tile in enumerate((taps[0], taps[1], taps[2], rot[...])):
        firsts = jnp.where(group == k, spin(tile, RIM * k), firsts)
        finals = jnp.where(group == k, spin(tile, RIM * k + RIM), finals)
    beside_near[count:] = jnp.where(even_axial, finals, firsts)
    beside_far[count:] = jnp.where(even_axial, firsts, finals)
    beside_near[count - 8 : count] = jnp.zeros((8, LANES), jnp.float32)
    beside_far[count - 8 : count] = jnp.zeros((8, LANES), jnp.float32)

    fields = [velocity.at[0], velocity.at[1], velocity.at[2], damping]
    for number, field in enumerate(fields):
        depth, start = DEPTHS[number], STARTS[number]
        for i in range(HALO - depth, HALO + pairs):
            if i < HALO:
                block = paired(lower[start + i - HALO + depth], upper[start + HALO - 1 - i])
            else:
                block = paired(field[i - HALO], field[cells - 1 - i + HALO])
            blocks[number, i] = block
            if (number, i) not in table:
                continue
            row, reach = table[number, i]
            rows = slice(row, row + reach)
            first, final = blocks[number, i, 0:reach], blocks[number, i, LANES - reach : LANES]
            beside_near[rows] = jnp.where(even_axial, final, first)
            beside_far[rows] = jnp.where(even_axial, first, final)


def basis_kernel(
    blocks,
    taps,
    rot,
    far,
    near,
    p0,
    p1,
    p2,
    s0,
    s1,
    s2,
    sums,
    v0,
    v1,
    v2,
    diag,
    rims,
    mirror,
    line,
    face,
    both,
):
    odd = lax.rem(lax.axis_index("radax"), 2)
    both[1 - odd] = near[...]
    both[odd] = far[...]
    before, after = both.at[0], both.at[1]
    pairs = blocks.shape[1] - HALO
    cells = 2 * pairs
    last = HALO + pairs - 1
    every = range(TILES + 2)
    place = lax.axis_index("radax")
    has_before, has_after = place > 0, place < lax.axis_size("radax") - 1
    lane = iota((8, LANES), 1)
    first_cell = lane % HALF == 0
    last_cell = lane % HALF == HALF - 1
    sign = jnp.where(lane < HALF, 1.0, -1.0)
    tenth = 0.1 * sign

    def walled(t, value):
        if t == 0:
            return jnp.where(has_before, value, 0.0)
        if t == TILES + 1:
            return jnp.where(has_after, value, 0.0)
        return value

    def seam(field):
        for t in every:
            field[last + 1, at(t)] = spin(field[last, at(t)], HALF)

    table, count = strips(pairs)
    shift = 6.0 - CENTER
    for number, field in enumerate((v0, v1, v2, diag)):
        for i in range(HALO - DEPTHS[number], last + 1):
            block = blocks[number, i]
            field[i, BODY] = block + shift if number == 3 else block
            if (number, i) not in table:
                continue
            for message, t in ((before, 0), (after, TILES + 1)):
                row, reach = table[number, i]
                value = walled(t, message[row : row + reach])
                value = value + shift if number == 3 else value
                row = FRONT - reach if t == 0 else FRONT + LANES
                field[i, row : row + reach] = value
    for field in (v0, v1, v2):
        seam(field)

    wide = cells + 6
    left = iota((STRIP, LANES), 1) < HALF
    for k in range(4):
        rims[k] = jnp.where(
            left, spin(after[count:], -RIM * k), spin(before[count:], -RIM - RIM * k)
        )
    for part in range(2):
        flux = jnp.zeros((wide, LANES), jnp.float32)
        for tap in range(3):
            if part == 0:
                flux += taps[tap, 0:wide] * rot[tap : tap + wide]
            else:
                flux += rims[tap, 0:wide] * rims[3, tap : tap + wide]
        mirror[2 : 2 + wide // 2] = flux[0 : wide // 2]
        for i in range(2, last + 1):
            mirror[HALF + i : HALF + i + 1] = flux[wide + 1 - i : wide + 2 - i]
        columns = mirror[...].T
        if part == 0:
            line[BODY] = columns
        else:
            line[FRONT + LANES : FRONT + LANES + 8] = columns[0:8]
            line[FRONT - 8 : FRONT] = columns[LANES - 8 : LANES]
    for i in range(2, last + 1):
        for t in every:
            face[i, at(t)] = spin(line[at(t)], -i)

    def radial(tile, inner):
        inward = jnp.where(first_cell, inner, spin(tile, 1))
        outward = jnp.where(last_cell, 0.0, spin(tile, -1))
        return inward, outward

    def advance(field, i, t, inner):
        x, lo, hi = field[i, at(t)], field[i - 1, at(t)], field[i + 1, at(t)]
        inward, outward = radial(x, inner)
        around = (field[i, at(t, -1)] + field[i, at(t, 1)]) + (inward + outward) + (lo + hi)
        wind = tenth * v0[i, at(t)]
        return walled(t, (0.4 * x + 0.1 * around) - wind * (hi - lo))

    def first_component(i, carry):
        for t in every:
            p0[i, at(t)] = advance(v0, i, t, 0.0)
        return carry

    def other_components(i, carry):
        for t in every:
            p1[i, at(t)] = advance(v1, i, t, face[i, at(t)])
            p2[i, at(t)] = advance(v2, i, t, 0.0)
        return carry

    def divergence(i, carry):
        for t in every:
            inward, outward = radial(p1[i, at(t)], face[i, at(t)])
            value = sign * (p0[i + 1, at(t)] - p0[i - 1, at(t)]) + (outward - inward)
            value = value + (p2[i, at(t, 1)] - p2[i, at(t, -1)])
            s0[i, at(t)] = walled(t, 0.5 * value)
        return carry

    def apply(field, i, t):
        x = field[i, at(t)]
        inward, outward = radial(x, 0.0)
        around = (field[i, at(t, -1)] + field[i, at(t, 1)]) + (inward + outward)
        around = around + (field[i - 1, at(t)] + field[i + 1, at(t)])
        return walled(t, diag[i, at(t)] * x - around)

    def second(i, carry):
        for t in every:
            s1[i, at(t)] = apply(s0, i, t)
        return carry

    def third(i, carry):
        for t in every:
            s2[i, at(t)] = apply(s1, i, t)
        return carry

    def products(i, carry):
        for t in range(1, TILES + 1):
            fourth = apply(s2, i, t)
            a, b, c = s0[i, at(t)], s1[i, at(t)], s2[i, at(t)]
            factors = ((a, a), (a, b), (b, b), (b, c), (c, c), (c, fourth))
            carry = tuple(s + x * y for s, (x, y) in zip(carry, factors))
        return carry

    lax.fori_loop(1, last + 1, first_component, 0, unroll=True)
    seam(p0)
    lax.fori_loop(2, last + 1, other_components, 0, unroll=True)
    lax.fori_loop(2, last + 1, divergence, 0, unroll=True)
    seam(s0)
    lax.fori_loop(3, last + 1, second, 0, unroll=True)
    seam(s1)
    lax.fori_loop(4, last + 1, third, 0, unroll=True)
    seam(s2)
    zero = jnp.zeros((8, LANES), jnp.float32)
    parts = lax.fori_loop(HALO, last + 1, products, (zero,) * 6, unroll=True)

    group = iota((1, LANES), 1) // 16
    packed = jnp.zeros((1, LANES), jnp.float32)
    for k, part in enumerate(parts):
        part = jnp.sum(part, axis=0, keepdims=True)
        for step in (64, 32, 16):
            part = part + pltpu.roll(part, step, 1)
        packed = jnp.where(group == k, part, packed)
    sums[...] = jnp.broadcast_to(packed[None], sums.shape)


def coefficients(nu):
    def product(x, y):
        total = 0.0
        for i, a in enumerate(x):
            for j, b in enumerate(y):
                total = total + a * b * nu[i + j]
        return total

    def energy(x):
        total = 0.0
        for i, a in enumerate(x):
            for j, b in enumerate(x):
                total = total + a * b * (nu[i + j + 1] + CENTER * nu[i + j])
        return total

    def image(x):
        out = [CENTER * a for a in x] + [0.0 * x[0]]
        return [out[0]] + [out[i + 1] + x[i] for i in range(len(x))]

    def length(norm, bottom):
        return jnp.clip(norm / bottom, 0.0624, 2.01)

    one = jnp.ones_like(nu[0])
    residual, direction, norm = [one], [one], nu[0]
    answer = [0.0 * one] * 3
    for step in range(3):
        alpha = length(norm, energy(direction))
        answer = [
            a + alpha * direction[i] if i < len(direction) else a for i, a in enumerate(answer)
        ]
        if step == 2:
            break
        moved = image(direction)
        residual = residual + [0.0 * one] * (len(moved) - len(residual))
        residual = [r - alpha * m for r, m in zip(residual, moved)]
        after = product(residual, residual)
        beta = after / norm
        padded = direction + [0.0 * one]
        direction = [r + beta * d for r, d in zip(residual, padded)]
        norm = after
    return answer


def project_kernel(sums, p0, p1, p2, s0, s1, s2, velocity, pressure, field, done):
    cells, rows = pressure.shape[0], pressure.shape[1]
    pairs = cells // 2
    last = HALO + pairs - 1
    lane = iota((8, LANES), 1)
    first_cell = lane % HALF == 0
    last_cell = lane % HALF == HALF - 1
    half = jnp.where(lane < HALF, 0.5, -0.5)
    total = jnp.sum(sums[...], axis=0)
    group = iota((1, LANES), 1) // 16
    nu = [jnp.sum(jnp.where(group == k, total, 0.0), axis=1, keepdims=True) for k in range(6)]
    c0, c1, c2 = coefficients(nu)

    def combine(i, carry):
        for t in range(TILES + 2):
            value = c0 * s0[i, at(t)] + c1 * s1[i, at(t)] + c2 * s2[i, at(t)]
            field[i, at(t)] = value
        return carry

    lax.fori_loop(HALO - 1, last + 1, combine, 0, unroll=True)
    for t in range(1, TILES + 1):
        field[last + 1, at(t)] = spin(field[last, at(t)], HALF)

    def gradient(i, carry):
        for t in range(1, TILES + 1):
            x = field[i, at(t)]
            inward = jnp.where(first_cell, 0.0, spin(x, 1))
            outward = jnp.where(last_cell, 0.0, spin(x, -1))
            around = half * (field[i + 1, at(t)] - field[i - 1, at(t)])
            along = 0.5 * (field[i, at(t, 1)] - field[i, at(t, -1)])
            own = slice(8 * t - 8, 8 * t)
            done[0, own] = p0[i, at(t)] - around
            done[1, own] = p1[i, at(t)] - 0.5 * (outward - inward)
            done[2, own] = p2[i, at(t)] - along
        for k in range(3):
            planes = done[k].T
            velocity[k, i - HALO] = planes[0:rows]
            velocity[k, last + pairs - i] = planes[rows:]
        planes = field[i, BODY].T
        pressure[i - HALO] = planes[0:rows]
        pressure[last + pairs - i] = planes[rows:]
        return carry

    lax.fori_loop(HALO, last + 1, gradient, 0, unroll=True)


def call(
    kernel, shapes, operands, scratch=(), spaces=None, outs=None, sems=0
):
    spec = lambda space: pl.BlockSpec(memory_space=space)
    spaces = spaces or [pltpu.VMEM] * len(operands)
    outs = outs or [pltpu.VMEM] * len(shapes)
    operands = [
        pltpu.with_memory_space_constraint(x, pltpu.HBM) if space is pltpu.HBM else x
        for x, space in zip(operands, spaces)
    ]
    buffers = [pltpu.VMEM(s, jnp.float32) for s in scratch]
    if sems:
        buffers.append(pltpu.SemaphoreType.DMA((sems,)))
    return pl.pallas_call(
        kernel,
        out_shape=[
            space(s, jnp.float32) if space is pltpu.HBM else jax.ShapeDtypeStruct(s, jnp.float32)
            for s, space in zip(shapes, outs)
        ],
        in_specs=[spec(space) for space in spaces],
        out_specs=[spec(space) for space in outs],
        scratch_shapes=buffers,
        compiler_params=pltpu.CompilerParams(vmem_limit_bytes=VMEM_LIMIT),
    )(*operands)


def trade(near, far, axis):
    count = lax.axis_size(axis)
    first = [(i, i ^ 1) for i in range(count)]
    second = [(i, (i + 2 * (i % 2) - 1) % count) for i in range(count)]
    return lax.ppermute(far, axis, second), lax.ppermute(near, axis, first)


def per_device(velocity, rotor_flux, correlation_weight, damping, offset):
    cells, rows = damping.shape[0], damping.shape[1]
    azim = lax.axis_size("azim")
    devices = azim * lax.axis_size("radax")
    plane = (rows, LANES)
    block = (LANES, LANES)
    pairs = cells // 2
    message = (PLANES + 1,) + plane
    near, far, spread, vel, damp = call(
        plane_kernel,
        [message, message, (azim, cells, LANES), velocity.shape, damping.shape],
        (velocity, damping, correlation_weight, rotor_flux),
        scratch=[(cells, LANES), (azim, cells, LANES)],
        spaces=[pltpu.HBM] * 4,
        outs=[pltpu.VMEM, pltpu.VMEM, pltpu.HBM, pltpu.VMEM, pltpu.VMEM],
        sems=18,
    )
    from_far, from_near = trade(near, far, "azim")
    turned = lax.all_to_all(spread, "azim", 0, 0, tiled=True)
    beside = (strips(pairs)[1] + STRIP, LANES)
    beside_near, beside_far, blocks, taps, rot = call(
        gather_kernel,
        [beside, beside, (4, HALO + pairs) + block, (3, cells + 8, LANES), (cells + 8, LANES)],
        (offset, vel, damp, near, from_near, from_far, turned),
        scratch=[(2,) + message],
        spaces=[pltpu.SMEM] + [pltpu.VMEM] * 6,
    )
    beside_from_far, beside_from_near = trade(beside_near, beside_far, "radax")
    field = (HALO + pairs + 1, TALL, LANES)
    *fields, sums = call(
        basis_kernel,
        [field] * 6 + [(devices, 1, LANES)],
        (blocks, taps, rot, beside_from_far, beside_from_near),
        scratch=[field] * 4
        + [(4, STRIP, LANES), block, (TALL, LANES), field, (2,) + beside],
    )
    sums = lax.all_to_all(sums, ("azim", "radax"), 0, 0, tiled=True)
    return call(
        project_kernel,
        [(3, cells) + plane, (cells,) + plane],
        (sums, *fields),
        scratch=[field, (3,) + block],
    )


def solution(mesh):
    in_specs = (
        P(None, "azim", None, "radax"),
        P("azim", "radax"),
        P(None, "azim", "radax"),
        P("azim", None, "radax"),
        P(),
    )
    out_specs = (P(None, "azim", None, "radax"), P("azim", None, "radax"))

    def run(*args):
        return tuple(per_device(*args))

    return jax.shard_map(run, mesh=mesh, in_specs=in_specs, out_specs=out_specs, check_vma=False)
```

```python
import jax
import jax.numpy as jnp
from jax import lax
from jax.experimental import pallas as pl
from jax.experimental.pallas import tpu as pltpu
from jax.sharding import PartitionSpec as P


CENTER = 8.0
HALO = 5
LANES = 128
HALF = 64
FRONT = 16
TALL = LANES + 2 * FRONT
TILES = LANES // 8
VMEM_LIMIT = 32 * 1024 * 1024
DEPTHS = (5, 4, 4, 2)
STARTS = (0, 5, 9, 13)
PLANES = 15
REACH = (4, 4, 5, 2)
LAG = (0, 1, 0, 3)
STRIP = 16
RIM = 8
BODY = slice(FRONT, FRONT + LANES)


def strips(pairs):
    table, row = {}, 0
    for i in range(HALO + pairs):
        for number in range(4):
            reach = max(min(i - LAG[number], REACH[number]), 0)
            if reach:
                table[number, i] = (row, reach)
            row += reach
    return table, row + -row % 8


def iota(shape, dim):
    return lax.broadcasted_iota(jnp.int32, shape, dim)


def spin(tile, steps):
    return pltpu.roll(tile, steps % LANES, 1) if steps % LANES else tile


def at(t, shift=0):
    start = FRONT - 8 + 8 * t + shift
    return slice(start, start + 8)


def paired(first, second):
    return jnp.concatenate([first, second], axis=0).T


def plane_kernel(
    velocity, damping, weight, rotor, near, far, spread, vel, damp, lines, ready, sems
):
    cells, rows = damping.shape[0], damping.shape[1]
    even = lax.rem(lax.axis_index("azim"), 2) == 0
    first = pltpu.make_async_copy(rotor, lines, sems.at[0])
    first.start()
    copies = []

    def copy(source, target):
        copies.append(pltpu.make_async_copy(source, target, sems.at[1 + len(copies)]))
        copies[-1].start()

    fields = [velocity.at[0], velocity.at[1], velocity.at[2], damping]
    for field, depth, start in zip(fields, DEPTHS, STARTS):
        target = slice(start, start + depth)
        copy(field.at[pl.ds(jnp.where(even, cells - depth, 0), depth)], near.at[target])
        copy(field.at[pl.ds(jnp.where(even, 0, cells - depth), depth)], far.at[target])
    for tap in range(3):
        target = slice(tap * cells, (tap + 1) * cells)
        copy(weight.at[tap], near.at[PLANES, target])
        copy(weight.at[tap], far.at[PLANES, target])
    copy(velocity, vel)
    copy(damping, damp)
    for message in (near, far):
        message[PLANES, 3 * cells : rows] = jnp.zeros((rows - 3 * cells, LANES), jnp.float32)
    first.wait()
    ready[...] = jnp.broadcast_to(lines[...][None], ready.shape)
    copy(ready, spread)
    for each in copies:
        each.wait()


def gather_kernel(
    offset,
    velocity,
    damping,
    mine,
    near,
    far,
    turned,
    beside_near,
    beside_far,
    blocks,
    taps,
    rot,
    halves,
):
    cells = damping.shape[0]
    pairs = cells // 2
    odd = lax.rem(lax.axis_index("azim"), 2)
    even_axial = lax.rem(lax.axis_index("radax"), 2) == 0
    halves[1 - odd] = near[...]
    halves[odd] = far[...]
    lower, upper = halves.at[0], halves.at[1]

    total = turned.shape[0] * cells
    begin = lax.axis_index("azim") * cells - offset[0] - 4 + 2 * total
    for k in range(cells + 8):
        source = lax.rem(begin + k, total)
        rot[k : k + 1] = turned[source // cells, pl.ds(lax.rem(source, cells), 1)]
    wide = cells + 6
    for tap in range(3):
        k = tap * cells
        taps[tap, 0:3] = lower[PLANES, k + cells - 3 : k + cells]
        taps[tap, 3 : 3 + cells] = mine[PLANES, k : k + cells]
        taps[tap, 3 + cells : wide] = upper[PLANES, k : k + 3]
        taps[tap, wide : wide + 2] = jnp.zeros((2, LANES), jnp.float32)

    table, count = strips(pairs)
    group = iota((STRIP, LANES), 1) // RIM
    firsts = finals = jnp.zeros((STRIP, LANES), jnp.float32)
    for k, tile in enumerate((taps[0], taps[1], taps[2], rot[...])):
        firsts = jnp.where(group == k, spin(tile, RIM * k), firsts)
        finals = jnp.where(group == k, spin(tile, RIM * k + RIM), finals)
    beside_near[count:] = jnp.where(even_axial, finals, firsts)
    beside_far[count:] = jnp.where(even_axial, firsts, finals)
    beside_near[count - 8 : count] = jnp.zeros((8, LANES), jnp.float32)
    beside_far[count - 8 : count] = jnp.zeros((8, LANES), jnp.float32)

    fields = [velocity.at[0], velocity.at[1], velocity.at[2], damping]
    for number, field in enumerate(fields):
        depth, start = DEPTHS[number], STARTS[number]
        for i in range(HALO - depth, HALO + pairs):
            if i < HALO:
                block = paired(lower[start + i - HALO + depth], upper[start + HALO - 1 - i])
            else:
                block = paired(field[i - HALO], field[cells - 1 - i + HALO])
            blocks[number, i] = block
            if (number, i) not in table:
                continue
            row, reach = table[number, i]
            rows = slice(row, row + reach)
            first, final = blocks[number, i, 0:reach], blocks[number, i, LANES - reach : LANES]
            beside_near[rows] = jnp.where(even_axial, final, first)
            beside_far[rows] = jnp.where(even_axial, first, final)


def basis_kernel(
    blocks,
    taps,
    rot,
    far,
    near,
    p0,
    p1,
    p2,
    s0,
    s1,
    s2,
    sums,
    v0,
    v1,
    v2,
    diag,
    rims,
    mirror,
    line,
    face,
    both,
):
    odd = lax.rem(lax.axis_index("radax"), 2)
    both[1 - odd] = near[...]
    both[odd] = far[...]
    before, after = both.at[0], both.at[1]
    pairs = blocks.shape[1] - HALO
    cells = 2 * pairs
    last = HALO + pairs - 1
    every = range(TILES + 2)
    place = lax.axis_index("radax")
    has_before, has_after = place > 0, place < lax.axis_size("radax") - 1
    lane = iota((8, LANES), 1)
    first_cell = lane % HALF == 0
    last_cell = lane % HALF == HALF - 1
    sign = jnp.where(lane < HALF, 1.0, -1.0)
    tenth = 0.1 * sign

    def walled(t, value):
        if t == 0:
            return jnp.where(has_before, value, 0.0)
        if t == TILES + 1:
            return jnp.where(has_after, value, 0.0)
        return value

    def seam(field):
        for t in every:
            field[last + 1, at(t)] = spin(field[last, at(t)], HALF)

    table, count = strips(pairs)
    shift = 6.0 - CENTER
    for number, field in enumerate((v0, v1, v2, diag)):
        for i in range(HALO - DEPTHS[number], last + 1):
            block = blocks[number, i]
            field[i, BODY] = block + shift if number == 3 else block
            if (number, i) not in table:
                continue
            for message, t in ((before, 0), (after, TILES + 1)):
                row, reach = table[number, i]
                value = walled(t, message[row : row + reach])
                value = value + shift if number == 3 else value
                row = FRONT - reach if t == 0 else FRONT + LANES
                field[i, row : row + reach] = value
    for field in (v0, v1, v2):
        seam(field)

    wide = cells + 6
    left = iota((STRIP, LANES), 1) < HALF
    for k in range(4):
        rims[k] = jnp.where(
            left, spin(after[count:], -RIM * k), spin(before[count:], -RIM - RIM * k)
        )
    for part in range(2):
        flux = jnp.zeros((wide, LANES), jnp.float32)
        for tap in range(3):
            if part == 0:
                flux += taps[tap, 0:wide] * rot[tap : tap + wide]
            else:
                flux += rims[tap, 0:wide] * rims[3, tap : tap + wide]
        mirror[2 : 2 + wide // 2] = flux[0 : wide // 2]
        for i in range(2, last + 1):
            mirror[HALF + i : HALF + i + 1] = flux[wide + 1 - i : wide + 2 - i]
        columns = mirror[...].T
        if part == 0:
            line[BODY] = columns
        else:
            line[FRONT + LANES : FRONT + LANES + 8] = columns[0:8]
            line[FRONT - 8 : FRONT] = columns[LANES - 8 : LANES]
    for i in range(2, last + 1):
        for t in every:
            face[i, at(t)] = spin(line[at(t)], -i)

    def radial(tile, inner):
        inward = jnp.where(first_cell, inner, spin(tile, 1))
        outward = jnp.where(last_cell, 0.0, spin(tile, -1))
        return inward, outward

    def advance(field, i, t, inner):
        x, lo, hi = field[i, at(t)], field[i - 1, at(t)], field[i + 1, at(t)]
        inward, outward = radial(x, inner)
        around = (field[i, at(t, -1)] + field[i, at(t, 1)]) + (inward + outward) + (lo + hi)
        wind = tenth * v0[i, at(t)]
        return walled(t, (0.4 * x + 0.1 * around) - wind * (hi - lo))

    def first_component(i, carry):
        for t in every:
            p0[i, at(t)] = advance(v0, i, t, 0.0)
        return carry

    def other_components(i, carry):
        for t in every:
            p1[i, at(t)] = advance(v1, i, t, face[i, at(t)])
            p2[i, at(t)] = advance(v2, i, t, 0.0)
        return carry

    def divergence(i, carry):
        for t in every:
            inward, outward = radial(p1[i, at(t)], face[i, at(t)])
            value = sign * (p0[i + 1, at(t)] - p0[i - 1, at(t)]) + (outward - inward)
            value = value + (p2[i, at(t, 1)] - p2[i, at(t, -1)])
            s0[i, at(t)] = walled(t, 0.5 * value)
        return carry

    def apply(field, i, t):
        x = field[i, at(t)]
        inward, outward = radial(x, 0.0)
        around = (field[i, at(t, -1)] + field[i, at(t, 1)]) + (inward + outward)
        around = around + (field[i - 1, at(t)] + field[i + 1, at(t)])
        return walled(t, diag[i, at(t)] * x - around)

    def second(i, carry):
        for t in every:
            s1[i, at(t)] = apply(s0, i, t)
        return carry

    def third(i, carry):
        for t in every:
            s2[i, at(t)] = apply(s1, i, t)
        return carry

    def products(i, carry):
        for t in range(1, TILES + 1):
            fourth = apply(s2, i, t)
            a, b, c = s0[i, at(t)], s1[i, at(t)], s2[i, at(t)]
            factors = ((a, a), (a, b), (b, b), (b, c), (c, c), (c, fourth))
            carry = tuple(s + x * y for s, (x, y) in zip(carry, factors))
        return carry

    lax.fori_loop(1, last + 1, first_component, 0, unroll=True)
    seam(p0)
    lax.fori_loop(2, last + 1, other_components, 0, unroll=True)
    lax.fori_loop(2, last + 1, divergence, 0, unroll=True)
    seam(s0)
    lax.fori_loop(3, last + 1, second, 0, unroll=True)
    seam(s1)
    lax.fori_loop(4, last + 1, third, 0, unroll=True)
    seam(s2)
    zero = jnp.zeros((8, LANES), jnp.float32)
    parts = lax.fori_loop(HALO, last + 1, products, (zero,) * 6, unroll=True)

    group = iota((1, LANES), 1) // 16
    packed = jnp.zeros((1, LANES), jnp.float32)
    for k, part in enumerate(parts):
        part = jnp.sum(part, axis=0, keepdims=True)
        for step in (64, 32, 16):
            part = part + pltpu.roll(part, step, 1)
        packed = jnp.where(group == k, part, packed)
    sums[...] = jnp.broadcast_to(packed[None], sums.shape)


def coefficients(nu):
    def product(x, y):
        total = 0.0
        for i, a in enumerate(x):
            for j, b in enumerate(y):
                total = total + a * b * nu[i + j]
        return total

    def energy(x):
        total = 0.0
        for i, a in enumerate(x):
            for j, b in enumerate(x):
                total = total + a * b * (nu[i + j + 1] + CENTER * nu[i + j])
        return total

    def image(x):
        out = [CENTER * a for a in x] + [0.0 * x[0]]
        return [out[0]] + [out[i + 1] + x[i] for i in range(len(x))]

    def length(norm, bottom):
        return jnp.clip(norm / bottom, 0.0624, 2.01)

    one = jnp.ones_like(nu[0])
    residual, direction, norm = [one], [one], nu[0]
    answer = [0.0 * one] * 3
    for step in range(3):
        alpha = length(norm, energy(direction))
        answer = [
            a + alpha * direction[i] if i < len(direction) else a for i, a in enumerate(answer)
        ]
        if step == 2:
            break
        moved = image(direction)
        residual = residual + [0.0 * one] * (len(moved) - len(residual))
        residual = [r - alpha * m for r, m in zip(residual, moved)]
        after = product(residual, residual)
        beta = after / norm
        padded = direction + [0.0 * one]
        direction = [r + beta * d for r, d in zip(residual, padded)]
        norm = after
    return answer


def project_kernel(sums, p0, p1, p2, s0, s1, s2, velocity, pressure, field, done):
    cells, rows = pressure.shape[0], pressure.shape[1]
    pairs = cells // 2
    last = HALO + pairs - 1
    lane = iota((8, LANES), 1)
    first_cell = lane % HALF == 0
    last_cell = lane % HALF == HALF - 1
    half = jnp.where(lane < HALF, 0.5, -0.5)
    total = jnp.sum(jnp.sum(sums[...], axis=0), axis=0, keepdims=True)
    group = iota((1, LANES), 1) // 16
    nu = [jnp.sum(jnp.where(group == k, total, 0.0), axis=1, keepdims=True) for k in range(6)]
    c0, c1, c2 = coefficients(nu)

    def combine(i, carry):
        for t in range(TILES + 2):
            value = c0 * s0[i, at(t)] + c1 * s1[i, at(t)] + c2 * s2[i, at(t)]
            field[i, at(t)] = value
        return carry

    lax.fori_loop(HALO - 1, last + 1, combine, 0, unroll=True)
    for t in range(1, TILES + 1):
        field[last + 1, at(t)] = spin(field[last, at(t)], HALF)

    def gradient(i, carry):
        for t in range(1, TILES + 1):
            x = field[i, at(t)]
            inward = jnp.where(first_cell, 0.0, spin(x, 1))
            outward = jnp.where(last_cell, 0.0, spin(x, -1))
            around = half * (field[i + 1, at(t)] - field[i - 1, at(t)])
            along = 0.5 * (field[i, at(t, 1)] - field[i, at(t, -1)])
            own = slice(8 * t - 8, 8 * t)
            done[0, own] = p0[i, at(t)] - around
            done[1, own] = p1[i, at(t)] - 0.5 * (outward - inward)
            done[2, own] = p2[i, at(t)] - along
        for k in range(3):
            planes = done[k].T
            velocity[k, i - HALO] = planes[0:rows]
            velocity[k, last + pairs - i] = planes[rows:]
        planes = field[i, BODY].T
        pressure[i - HALO] = planes[0:rows]
        pressure[last + pairs - i] = planes[rows:]
        return carry

    lax.fori_loop(HALO, last + 1, gradient, 0, unroll=True)


def call(
    kernel, shapes, operands, scratch=(), spaces=None, outs=None, sems=0
):
    spec = lambda space: pl.BlockSpec(memory_space=space)
    spaces = spaces or [pltpu.VMEM] * len(operands)
    outs = outs or [pltpu.VMEM] * len(shapes)
    operands = [
        pltpu.with_memory_space_constraint(x, pltpu.HBM) if space is pltpu.HBM else x
        for x, space in zip(operands, spaces)
    ]
    buffers = [pltpu.VMEM(s, jnp.float32) for s in scratch]
    if sems:
        buffers.append(pltpu.SemaphoreType.DMA((sems,)))
    return pl.pallas_call(
        kernel,
        out_shape=[
            space(s, jnp.float32) if space is pltpu.HBM else jax.ShapeDtypeStruct(s, jnp.float32)
            for s, space in zip(shapes, outs)
        ],
        in_specs=[spec(space) for space in spaces],
        out_specs=[spec(space) for space in outs],
        scratch_shapes=buffers,
        compiler_params=pltpu.CompilerParams(vmem_limit_bytes=VMEM_LIMIT),
    )(*operands)


def trade(near, far, axis):
    count = lax.axis_size(axis)
    first = [(i, i ^ 1) for i in range(count)]
    second = [(i, (i + 2 * (i % 2) - 1) % count) for i in range(count)]
    return lax.ppermute(far, axis, second), lax.ppermute(near, axis, first)


def per_device(velocity, rotor_flux, correlation_weight, damping, offset):
    cells, rows = damping.shape[0], damping.shape[1]
    azim = lax.axis_size("azim")
    devices = azim * lax.axis_size("radax")
    plane = (rows, LANES)
    block = (LANES, LANES)
    pairs = cells // 2
    message = (PLANES + 1,) + plane
    near, far, spread, vel, damp = call(
        plane_kernel,
        [message, message, (azim, cells, LANES), velocity.shape, damping.shape],
        (velocity, damping, correlation_weight, rotor_flux),
        scratch=[(cells, LANES), (azim, cells, LANES)],
        spaces=[pltpu.HBM] * 4,
        outs=[pltpu.VMEM, pltpu.VMEM, pltpu.HBM, pltpu.VMEM, pltpu.VMEM],
        sems=18,
    )
    from_far, from_near = trade(near, far, "azim")
    turned = lax.all_to_all(spread, "azim", 0, 0, tiled=True)
    beside = (strips(pairs)[1] + STRIP, LANES)
    beside_near, beside_far, blocks, taps, rot = call(
        gather_kernel,
        [beside, beside, (4, HALO + pairs) + block, (3, cells + 8, LANES), (cells + 8, LANES)],
        (offset, vel, damp, near, from_near, from_far, turned),
        scratch=[(2,) + message],
        spaces=[pltpu.SMEM] + [pltpu.VMEM] * 6,
    )
    beside_from_far, beside_from_near = trade(beside_near, beside_far, "radax")
    field = (HALO + pairs + 1, TALL, LANES)
    *fields, sums = call(
        basis_kernel,
        [field] * 6 + [(devices // 8, 8, LANES)],
        (blocks, taps, rot, beside_from_far, beside_from_near),
        scratch=[field] * 4
        + [(4, STRIP, LANES), block, (TALL, LANES), field, (2,) + beside],
    )
    sums = sums.reshape(devices, 1, LANES)
    sums = lax.all_to_all(sums, ("azim", "radax"), 0, 0, tiled=True)
    sums = sums.reshape(devices // 8, 8, LANES)
    return call(
        project_kernel,
        [(3, cells) + plane, (cells,) + plane],
        (sums, *fields),
        scratch=[field, (3,) + block],
    )


def solution(mesh):
    in_specs = (
        P(None, "azim", None, "radax"),
        P("azim", "radax"),
        P(None, "azim", "radax"),
        P("azim", None, "radax"),
        P(),
    )
    out_specs = (P(None, "azim", None, "radax"), P("azim", None, "radax"))

    def run(*args):
        return tuple(per_device(*args))

    return jax.shard_map(run, mesh=mesh, in_specs=in_specs, out_specs=out_specs, check_vma=False)
```
